256 devices in a mesh: src: 8 (over z), tgt: 32 (over x, y, core).
Axes of the slice: x: 4, y: 4, z: 8, core: 2. Of those that a mesh axis runs over, the one named last changes fastest.
Arguments:
- src_features: bfloat16 [262144, 32], P('src'), may hold values from -12 to 12
- tgt_features: bfloat16 [524288, 32], P('tgt'), may hold values from -4.5 to 4.5
- tgt_potential: float32 [524288], P('tgt'), may hold values from -12 to 12
- src_log_weight: float32 [262144], P('src'), may hold values from -1 to 1
- tgt_log_weight: float32 [524288], P('tgt'), may hold values from -1 to 1
- tile_ids: int32 [8, 32, 8], P('src', 'tgt'), may hold values from 0 to 127, as said below
- tile_level: int32 [8, 32, 8], P('src', 'tgt'), may hold values from 0 to 3
- tile_count: int32 [8, 32], P('src', 'tgt'), may hold values from 2 to 8
Outputs:
- src_potential: float32 [262144], P('src')
- new_tgt_potential: float32 [524288], P('tgt')
The draws below stay inside these ranges and needn't reach their ends.
Inputs may be any that keep to these rules, and one draw needn't show every extreme that they name: For device (s, t) the first tile_count[s, t] entries of tile_ids[s, t] are distinct; later entries are ignored. Every source block and every target block lies in some listed tile.
All inputs are finite; a program needn't handle non-finite values.
Results may differ from the reference program's by a relative error of at most 0.0003.
Values sent between devices are 32-bit elements; how exact they have to be, the bound alone decides.
No kernel may reach another device: no remote copies, remote signals or barrier semaphores. Data moves between devices by JAX's collectives and lax.ppermute only.
A program may use at most 64 MiB of HBM per device.

```python
import jax
import jax.numpy as jnp
from jax import lax

D = 32
BLK = 2048
SB_DEV = 16
TB_DEV = 8
MAXT = 8
NS = 262144
NT = 524288
N_SRC = 8
N_TGT = 32


def forced_count():
    return max((SB_DEV + N_TGT - 1) // N_TGT, (TB_DEV + N_SRC - 1) // N_SRC)


def listing(key):
    id_key = jax.random.fold_in(key, 11)
    forced = forced_count()
    pairs = SB_DEV * TB_DEV
    keys = jax.random.split(id_key, N_SRC * N_TGT)
    ranks = jax.vmap(lambda single: jax.random.permutation(single, pairs))(keys).reshape(N_SRC, N_TGT, pairs)
    priority = ranks.astype(jnp.int32) + forced
    src_grid = jnp.arange(N_SRC, dtype=jnp.int32)[:, None]
    tgt_grid = jnp.arange(N_TGT, dtype=jnp.int32)[None, :]
    pair_grid = jnp.arange(pairs, dtype=jnp.int32)
    for rank_no in range(forced):
        src_block = (forced * tgt_grid + rank_no) % SB_DEV
        tgt_block = (forced * src_grid + rank_no) % TB_DEV
        wanted = src_block * TB_DEV + tgt_block
        priority = jnp.where(pair_grid[None, None, :] == wanted[:, :, None], rank_no, priority)
    order = jnp.argsort(priority, axis=2, stable=True)
    listed_ids = order[:, :, :MAXT].astype(jnp.int32)
    count_key = jax.random.fold_in(key, 12)
    least = forced + (MAXT - forced) // 4
    first_key, second_key, third_key = jax.random.split(count_key, 3)
    heavy = jax.random.randint(first_key, (N_SRC * N_TGT,), 0, 8)
    light = jax.random.randint(second_key, (N_SRC * N_TGT,), least, forced + (MAXT - forced) // 2 + 1)
    counts = jnp.where(heavy == 0, MAXT, light)
    busiest = jax.random.randint(third_key, (), 0, N_SRC * N_TGT)
    counts = jnp.where(jnp.arange(N_SRC * N_TGT) == busiest, MAXT, counts)
    lowest = jax.random.randint(jax.random.fold_in(third_key, 5), (), 0, N_SRC * N_TGT)
    counts = jnp.where((jnp.arange(N_SRC * N_TGT) == lowest) & (lowest != busiest), least, counts)
    return (listed_ids, counts.reshape(N_SRC, N_TGT).astype(jnp.int32))


def block_centres(key):
    centre_key = jax.random.fold_in(key, 21)
    centres = jax.random.normal(centre_key, (SB_DEV * N_SRC, D), jnp.float32)
    return 0.7 * jnp.clip(centres, -4.0, 4.0)


def home_blocks(key):
    listed_ids, listed_counts = listing(key)
    src_blocks = SB_DEV * N_SRC
    tgt_blocks = TB_DEV * N_TGT
    src_grid = jnp.arange(N_SRC, dtype=jnp.int32)[:, None, None]
    tgt_grid = jnp.arange(N_TGT, dtype=jnp.int32)[None, :, None]
    row_block = jnp.broadcast_to(src_grid * SB_DEV + listed_ids // TB_DEV, listed_ids.shape).reshape(-1)
    col_block = jnp.broadcast_to(tgt_grid * TB_DEV + listed_ids % TB_DEV, listed_ids.shape).reshape(-1)
    valid = (jnp.arange(MAXT, dtype=jnp.int32)[None, None, :] < listed_counts[:, :, None]).astype(jnp.int32).reshape(-1)
    listed = jnp.zeros((src_blocks, tgt_blocks), jnp.int32).at[row_block, col_block].max(valid)
    listed_total = jnp.maximum(jnp.sum(listed, axis=0), 1)
    lookup = jnp.argsort(1 - listed.T, axis=1, stable=True).astype(jnp.int32)
    pick_key = jax.random.fold_in(key, 22)
    shuffles = jax.vmap(lambda single: jax.random.permutation(single, BLK))(jax.random.split(pick_key, tgt_blocks)).astype(jnp.int32)
    chosen = shuffles % listed_total[:, None]
    home_block = jnp.take_along_axis(lookup, chosen, axis=1)
    return home_block.reshape(NT)


def draw_src_features(key, part):
    centres = block_centres(key)
    key = jax.random.fold_in(key, 13)
    noise_key, scale_key = jax.random.split(key, 2)
    blocks = SB_DEV * N_SRC
    noise = jnp.clip(jax.random.normal(noise_key, (blocks, BLK, D), jnp.float32), -4.0, 4.0)
    spread = jnp.exp(jax.random.uniform(scale_key, (blocks, 1, 1), jnp.float32, jnp.log(0.15), jnp.log(0.35)))
    values = centres[:, None, :] + spread * noise
    return values.reshape(NS, D).astype(jnp.bfloat16)


def draw_tgt_features(key, part):
    centres = block_centres(key)
    home_block = home_blocks(key)
    key = jax.random.fold_in(key, 14)
    noise_key, scale_key = jax.random.split(key)
    noise = jnp.clip(jax.random.normal(noise_key, (NT, D), jnp.float32), -4.0, 4.0)
    spread = jnp.exp(jax.random.uniform(scale_key, (NT, 1), jnp.float32, jnp.log(0.15), jnp.log(0.35)))
    values = centres[home_block] + spread * noise
    return values.astype(jnp.bfloat16)


def draw_tile_ids(key, part):
    listed_ids, listed_counts = listing(key)
    return listed_ids


def draw_tile_count(key, part):
    listed_ids, listed_counts = listing(key)
    return listed_counts


def with_ends(values, stream_key, smallest, largest):
    shape = values.shape
    place = [jax.random.randint(jax.random.fold_in(stream_key, axis), (), 0, shape[axis]) for axis in range(len(shape))]
    values = values.at[tuple(place)].set(smallest)
    longest = shape.index(max(shape))
    place[longest] = (place[longest] + 1) % shape[longest]
    return values.at[tuple(place)].set(largest)


def level_of(key, dims, pieces, low, largest):
    loudness = 1.0
    for dim, shards_of in pieces:
        heights = jax.random.uniform(jax.random.fold_in(jax.random.fold_in(key, 6), dim), (shards_of,), jnp.float32, low / len(pieces), largest / len(pieces))
        loudness = loudness * jnp.repeat(jnp.exp(heights), dims[dim] // shards_of).reshape((-1,) + (1,) * (len(dims) - 1 - dim))
    return loudness


def centred(rng, extent, width, bound, shards=(), kind=jnp.bfloat16):
    result = width * jax.random.normal(rng, extent, jnp.float32)
    if shards:
        result = result * level_of(rng, extent, shards, -0.22, 0.18)
    return jnp.clip(result, -bound, bound).astype(kind)


def setup_inputs(seed: int = 0) -> dict:
    splits = jax.random.split(jax.random.key(seed), 9)
    return {
        "src_features": draw_src_features(jax.random.fold_in(splits[8], 71), 0),
        "tgt_features": draw_tgt_features(jax.random.fold_in(splits[8], 71), 0),
        "tgt_potential": centred(splits[2], (NT,), 2.0, 12.0, ((0, 32),), jnp.float32),
        "src_log_weight": jnp.clip(jax.random.uniform(splits[3], (NS,), jnp.float32, -1.0, 1.0) * level_of(splits[3], (NS,), ((0, 8),), -0.4, 0.0), -1.0, 1.0),
        "tgt_log_weight": jnp.clip(jax.random.uniform(splits[4], (NT,), jnp.float32, -1.0, 1.0) * level_of(splits[4], (NT,), ((0, 32),), -0.4, 0.0), -1.0, 1.0),
        "tile_ids": draw_tile_ids(jax.random.fold_in(splits[8], 71), 0),
        "tile_level": with_ends(jax.random.randint(splits[6], (N_SRC, N_TGT, MAXT), 0, 4), jax.random.fold_in(splits[6], 1), 0, 3).astype(jnp.int32),
        "tile_count": draw_tile_count(jax.random.fold_in(splits[8], 71), 0),
    }


VERY_LOW = -1.0e30


def pair_combine(first, second):
    maxima = jnp.maximum(first[0], second[0])
    return maxima, first[1] * jnp.exp(first[0] - maxima) + second[1] * jnp.exp(second[0] - maxima)


def tile_scaled(src_features, src_norm, tgt_features, tgt_norm, row_start, col_start, weight):
    src_rows = lax.dynamic_slice_in_dim(src_features, row_start, BLK, 0)
    tgt_rows = lax.dynamic_slice_in_dim(tgt_features, col_start, BLK, 0)
    src_part = lax.dynamic_slice_in_dim(src_norm, row_start, BLK, 0)
    tgt_part = lax.dynamic_slice_in_dim(tgt_norm, col_start, BLK, 0)
    cross_dot = jnp.dot(src_rows, tgt_rows.T, preferred_element_type=jnp.float32)
    return weight * (src_part[:, None] + tgt_part[None, :] - 2.0 * cross_dot)


def reference(src_features, tgt_features, tgt_potential, src_log_weight, tgt_log_weight, tile_ids, tile_level, tile_count):
    src_norm = jnp.sum(jnp.square(src_features.astype(jnp.float32)), axis=1)
    tgt_norm = jnp.sum(jnp.square(tgt_features.astype(jnp.float32)), axis=1)

    def tile_info(device, slot_index):
        src_index = device // N_TGT
        tgt_index = device % N_TGT
        tile_id = tile_ids[src_index, tgt_index, slot_index]
        row_start = ((src_index * SB_DEV + tile_id // TB_DEV) * BLK).astype(jnp.int32)
        col_start = ((tgt_index * TB_DEV + tile_id % TB_DEV) * BLK).astype(jnp.int32)
        weight = 0.125 * jnp.exp2(tile_level[src_index, tgt_index, slot_index].astype(jnp.float32))
        return row_start, col_start, weight

    def row_device(device, carry):
        def row_tile(slot_index, inner):
            peak_run, total_run = inner
            row_start, col_start, weight = tile_info(device, slot_index)
            scaled = tile_scaled(src_features, src_norm, tgt_features, tgt_norm, row_start, col_start, weight)
            scores = lax.dynamic_slice_in_dim(tgt_potential, col_start, BLK, 0)[None, :] - scaled
            tile_peak = jnp.max(scores, axis=1)
            tile_total = jnp.sum(jnp.exp(scores - tile_peak[:, None]), axis=1)
            merged = pair_combine((lax.dynamic_slice_in_dim(peak_run, row_start, BLK, 0), lax.dynamic_slice_in_dim(total_run, row_start, BLK, 0)), (tile_peak, tile_total))
            return (lax.dynamic_update_slice_in_dim(peak_run, merged[0], row_start, 0), lax.dynamic_update_slice_in_dim(total_run, merged[1], row_start, 0))
        listed = tile_count[device // N_TGT, device % N_TGT]
        return lax.fori_loop(0, listed, row_tile, carry)

    start_rows = (jnp.full((NS,), VERY_LOW, jnp.float32), jnp.zeros((NS,), jnp.float32))
    peak_rows, total_rows = lax.fori_loop(0, N_SRC * N_TGT, row_device, start_rows)
    src_potential = src_log_weight - (peak_rows + jnp.log(total_rows))

    def col_device(device, carry):
        def col_tile(slot_index, inner):
            peak_run, total_run = inner
            row_start, col_start, weight = tile_info(device, slot_index)
            scaled = tile_scaled(src_features, src_norm, tgt_features, tgt_norm, row_start, col_start, weight)
            scores = lax.dynamic_slice_in_dim(src_potential, row_start, BLK, 0)[:, None] - scaled
            tile_peak = jnp.max(scores, axis=0)
            tile_total = jnp.sum(jnp.exp(scores - tile_peak[None, :]), axis=0)
            merged = pair_combine((lax.dynamic_slice_in_dim(peak_run, col_start, BLK, 0), lax.dynamic_slice_in_dim(total_run, col_start, BLK, 0)), (tile_peak, tile_total))
            return (lax.dynamic_update_slice_in_dim(peak_run, merged[0], col_start, 0), lax.dynamic_update_slice_in_dim(total_run, merged[1], col_start, 0))
        listed = tile_count[device // N_TGT, device % N_TGT]
        return lax.fori_loop(0, listed, col_tile, carry)

    start_cols = (jnp.full((NT,), VERY_LOW, jnp.float32), jnp.zeros((NT,), jnp.float32))
    peak_cols, total_cols = lax.fori_loop(0, N_SRC * N_TGT, col_device, start_cols)
    new_tgt_potential = tgt_log_weight - (peak_cols + jnp.log(total_cols))
    return (src_potential, new_tgt_potential)
```

```python
import functools

import jax
import jax.numpy as jnp
from jax import lax
from jax.experimental import pallas as pl
from jax.experimental.pallas import tpu as pltpu
from jax.sharding import PartitionSpec as P

BLK = 2048
TB_DEV = 8
LANES = 128
DEPTH = 128
CHUNK = 256
LOG2E = 1.4426950408889634
LN2 = 0.6931471805599453
EMPTY = -1e30
MARGIN = 60.0
ROW_LIMIT = 2.0**120
UP = 100.0
COL_LIMIT = 2.0**-90
F32 = jnp.float32
BF16 = jnp.bfloat16


def split3(x):
    high = x.astype(BF16)
    rest = x - high.astype(F32)
    mid = rest.astype(BF16)
    low = rest - mid.astype(F32)
    return high.astype(F32), mid.astype(F32), low


def stacked(pieces):
    row = lax.broadcasted_iota(jnp.int32, (16, BLK), 0)
    out = jnp.zeros((16, BLK), F32)
    for index, piece in enumerate(pieces):
        out = jnp.where(row == index, piece, out)
    return out.astype(BF16)


def block(index):
    return pl.ds(pl.multiple_of(index * BLK, BLK), BLK)


def weight_of(level):
    return jnp.where(
        level == 0, 0.125, jnp.where(level == 1, 0.25, jnp.where(level == 2, 0.5, 1.0))
    ).astype(F32)


def prep_tgt(tgt_ref, pot_ref, rep_ref, index):
    raw = tgt_ref[:, block(index)]
    cells = raw.astype(F32)
    norm = jnp.sum(cells * cells, axis=0, keepdims=True)
    extra = stacked(
        [*split3(-LOG2E * norm), *split3(LOG2E * pot_ref[:, block(index)]), 1.0, 1.0, 1.0]
    )
    full = jnp.concatenate([raw, raw, raw, extra, jnp.zeros((16, BLK), BF16)], axis=0)
    rep_ref[block(index), :] = full.T


def prep_src(src_ref, rhs_ref, index, weight):
    cells = src_ref[:, block(index)].astype(F32)
    norm = jnp.sum(cells * cells, axis=0, keepdims=True)
    high, mid, low = split3(cells * (2.0 * LOG2E * weight))
    rhs_ref[0:32, :] = high.astype(BF16)
    rhs_ref[32:64, :] = mid.astype(BF16)
    rhs_ref[64:96, :] = low.astype(BF16)
    return (LOG2E * weight) * norm


def set_extra(rhs_ref, weight, term):
    rhs_ref[96:112, :] = stacked([weight, weight, weight, 1.0, 1.0, 1.0, *split3(term)])


def scores(rep_ref, rhs_ref, row, col):
    return jnp.dot(
        rep_ref[pl.ds(pl.multiple_of(row, CHUNK), CHUNK), :],
        rhs_ref[:, col : col + CHUNK],
        preferred_element_type=F32,
    )


def log_add(first, second):
    peak = jnp.maximum(first, second)
    return peak + jnp.log2(jnp.exp2(first - peak) + jnp.exp2(second - peak))


def row_kernel(ids, levels, count, tgt_ref, pot_ref, src_ref, lse_ref, rep_ref, rhs_ref, top_ref):
    rhs_ref[112:128, :] = jnp.zeros((16, BLK), BF16)

    def prep(index, carry):
        prep_tgt(tgt_ref, pot_ref, rep_ref, index)
        return carry

    lax.fori_loop(0, TB_DEV, prep, 0)

    def sums(start, col):
        total = jnp.zeros((8, CHUNK), F32)
        for row in range(0, BLK, CHUNK):
            part = jnp.exp2(scores(rep_ref, rhs_ref, start + row, col))
            total = total + jnp.sum(part.reshape(CHUNK // 8, 8, CHUNK), axis=0)
        return jnp.sum(total, axis=0, keepdims=True)

    def merge(src_block, col, value):
        cols = pl.ds(pl.multiple_of(src_block * BLK + col, CHUNK), CHUNK)
        lse_ref[:, cols] = log_add(lse_ref[:, cols], value)

    def tile(slot, carry):
        src_block = ids[slot] // TB_DEV
        tgt_block = ids[slot] % TB_DEV
        weight = weight_of(levels[slot])
        norm = prep_src(src_ref, rhs_ref, src_block, weight)
        set_extra(rhs_ref, weight, jnp.zeros((1, BLK), F32))
        start = tgt_block * BLK
        mean = jnp.dot(
            jnp.ones((16, BLK), BF16), rep_ref[block(tgt_block), :], preferred_element_type=F32
        ) * (1.0 / BLK)
        shift = MARGIN + jnp.dot(mean.astype(BF16), rhs_ref[...], preferred_element_type=F32)[0:1]
        set_extra(rhs_ref, weight, -shift)
        base = shift - norm
        for col in range(0, BLK, CHUNK):
            total = sums(start, col)
            top_ref[:, col : col + CHUNK] = jnp.maximum(top_ref[:, col : col + CHUNK], total)
            merge(src_block, col, base[:, col : col + CHUNK] + jnp.log2(total))
        return carry

    def safe_tile(slot, carry):
        src_block = ids[slot] // TB_DEV
        weight = weight_of(levels[slot])
        norm = prep_src(src_ref, rhs_ref, src_block, weight)
        set_extra(rhs_ref, weight, jnp.zeros((1, BLK), F32))
        start = ids[slot] % TB_DEV * BLK
        for col in range(0, BLK, CHUNK):

            def peak_part(step, peak):
                part = scores(rep_ref, rhs_ref, start + step * CHUNK, col)
                return jnp.maximum(peak, jnp.max(part.reshape(CHUNK // 8, 8, CHUNK), axis=0))

            peak = lax.fori_loop(0, BLK // CHUNK, peak_part, jnp.full((8, CHUNK), EMPTY, F32))
            peak = jnp.max(peak, axis=0, keepdims=True)

            def sum_part(step, total):
                part = jnp.exp2(scores(rep_ref, rhs_ref, start + step * CHUNK, col) - peak)
                return total + jnp.sum(part.reshape(CHUNK // 8, 8, CHUNK), axis=0)

            total = lax.fori_loop(0, BLK // CHUNK, sum_part, jnp.zeros((8, CHUNK), F32))
            total = jnp.sum(total, axis=0, keepdims=True)
            merge(src_block, col, peak - norm[:, col : col + CHUNK] + jnp.log2(total))
        return carry

    lse_ref[...] = jnp.full(lse_ref.shape, EMPTY, F32)
    top_ref[...] = jnp.zeros(top_ref.shape, F32)
    lax.fori_loop(0, count[0], tile, 0)

    @pl.when(jnp.logical_not(jnp.max(top_ref[...]) < ROW_LIMIT))
    def _():
        lse_ref[...] = jnp.full(lse_ref.shape, EMPTY, F32)
        lax.fori_loop(0, count[0], safe_tile, 0)


def col_kernel(ids, levels, count, rep_ref, src_ref, sp_ref, lse_ref, rhs_ref, wide_ref):
    rhs_ref[112:128, :] = jnp.zeros((16, BLK), BF16)

    def prep(slot):
        src_block = ids[slot] // TB_DEV
        weight = weight_of(levels[slot])
        norm = prep_src(src_ref, rhs_ref, src_block, weight)
        set_extra(rhs_ref, weight, sp_ref[:, block(src_block)] - norm + (UP - LOG2E))
        return ids[slot] % TB_DEV * BLK

    def tile(slot, carry):
        start = prep(slot)
        for row in range(0, BLK, CHUNK):
            total = jnp.zeros((CHUNK, LANES), F32)
            for col in range(0, BLK, CHUNK):
                part = jnp.exp2(scores(rep_ref, rhs_ref, start + row, col))
                for lane in range(0, CHUNK, LANES):
                    total = total + part[:, lane : lane + LANES]
            cols = pl.ds(pl.multiple_of(start + row, CHUNK), CHUNK)
            lse_ref[:, cols] = lse_ref[:, cols] + jnp.sum(total.T, axis=0, keepdims=True)
        return carry

    def safe_tile(slot, carry):
        start = prep(slot)

        def step(index, inner):
            row = start + index * CHUNK
            peak = jnp.full((CHUNK, LANES), EMPTY, F32)
            for col in range(0, BLK, CHUNK):
                part = scores(rep_ref, rhs_ref, row, col)
                for lane in range(0, CHUNK, LANES):
                    peak = jnp.maximum(peak, part[:, lane : lane + LANES])
            total = jnp.zeros((CHUNK, LANES), F32)
            for col in range(0, BLK, CHUNK):
                part = scores(rep_ref, rhs_ref, row, col)
                for lane in range(0, CHUNK, LANES):
                    total = total + jnp.exp2(part[:, lane : lane + LANES] - peak)
            rows = pl.ds(pl.multiple_of(row, CHUNK), CHUNK)
            wide_ref[rows, :] = log_add(wide_ref[rows, :], peak + jnp.log2(total))
            return inner

        lax.fori_loop(0, BLK // CHUNK, step, 0)
        return carry

    def lowest(slot, low):
        return jnp.minimum(low, lse_ref[:, block(ids[slot] % TB_DEV)])

    lse_ref[...] = jnp.zeros(lse_ref.shape, F32)
    lax.fori_loop(0, count[0], tile, 0)
    low = lax.fori_loop(0, count[0], lowest, jnp.full((1, BLK), 1.0, F32))
    sums = lse_ref[...]
    lse_ref[...] = jnp.where(sums > 0.0, jnp.log2(sums), EMPTY)

    @pl.when(jnp.logical_not(jnp.min(low) >= COL_LIMIT))
    def _():
        wide_ref[...] = jnp.full(wide_ref.shape, EMPTY, F32)
        lax.fori_loop(0, count[0], safe_tile, 0)

        def narrow(index, inner):
            cols = pl.ds(pl.multiple_of(index * CHUNK, CHUNK), CHUNK)
            wide = wide_ref[cols, :].T
            peak = jnp.max(wide, axis=0, keepdims=True)
            lse_ref[:, cols] = peak + jnp.log2(
                jnp.sum(jnp.exp2(wide - peak), axis=0, keepdims=True)
            )
            return inner

        lax.fori_loop(0, wide_ref.shape[0] // CHUNK, narrow, 0)


WHOLE = pl.BlockSpec(memory_space=pltpu.VMEM)
SCALAR = pl.BlockSpec(memory_space=pltpu.SMEM)
PARAMS = pltpu.CompilerParams(vmem_limit_bytes=56 * 2**20)


def row_pass(ids, levels, count, tgt, pot, src):
    return pl.pallas_call(
        row_kernel,
        out_shape=(
            jax.ShapeDtypeStruct((1, src.shape[1]), F32),
            jax.ShapeDtypeStruct((tgt.shape[1], DEPTH), BF16),
        ),
        in_specs=[SCALAR, SCALAR, SCALAR, WHOLE, WHOLE, WHOLE],
        out_specs=(WHOLE, WHOLE),
        scratch_shapes=[pltpu.VMEM((DEPTH, BLK), BF16), pltpu.VMEM((1, BLK), F32)],
        compiler_params=PARAMS,
        name="row_pass",
    )(ids, levels, count, tgt, pot, src)


def col_pass(ids, levels, count, rep, src, sp):
    return pl.pallas_call(
        col_kernel,
        out_shape=jax.ShapeDtypeStruct((1, rep.shape[0]), F32),
        in_specs=[SCALAR, SCALAR, SCALAR, WHOLE, WHOLE, WHOLE],
        out_specs=WHOLE,
        scratch_shapes=[
            pltpu.VMEM((DEPTH, BLK), BF16),
            pltpu.VMEM((rep.shape[0], LANES), F32),
        ],
        compiler_params=PARAMS,
        name="col_pass",
    )(ids, levels, count, rep, src, sp)


def log_sum(parts):
    peak = functools.reduce(jnp.maximum, parts)
    return peak + jnp.log2(sum(jnp.exp2(part - peak) for part in parts))


def exchanged(value, axis, masks):
    size = lax.axis_size(axis)
    parts = [
        lax.ppermute(value, axis, [(i, i ^ mask) for i in range(size)]) for mask in masks
    ]
    return log_sum([value, *parts])


def local(src, tgt, pot, src_log, tgt_log, tile_ids, tile_level, tile_count):
    ids, levels, count = tile_ids[0, 0], tile_level[0, 0], tile_count[0]
    src_t, tgt_t = src.T, tgt.T
    row_lse, rep = row_pass(ids, levels, count, tgt_t, pot[None], src_t)

    core = lax.axis_index("tgt") % 2
    swap = [(i, i ^ 1) for i in range(lax.axis_size("tgt"))]
    halves = row_lse.reshape(2, -1)
    kept = lax.dynamic_index_in_dim(halves, core, 0, False)
    sent = lax.dynamic_index_in_dim(halves, 1 - core, 0, False)
    half = log_sum([kept, lax.ppermute(sent, "tgt", swap)])
    half = exchanged(half, "tgt", (2, 4, 6))
    half = exchanged(half, "tgt", (8, 16, 24))
    src_half = lax.dynamic_index_in_dim(src_log.reshape(2, -1), core, 0, False)
    own = LOG2E * src_half - half
    other = lax.ppermute(own, "tgt", swap)
    sp = jnp.where(core == 0, jnp.concatenate([own, other]), jnp.concatenate([other, own]))

    col_lse = col_pass(ids, levels, count, rep, src_t, sp[None])[0]
    col_lse = exchanged(col_lse, "src", (1, 2, 3))
    col_lse = exchanged(col_lse, "src", (7,))
    new_pot = tgt_log + pot - (LN2 * (col_lse - UP) + 1.0)
    return LN2 * sp, new_pot


def solution(mesh):
    placed = (
        P("src", None),
        P("tgt", None),
        P("tgt"),
        P("src"),
        P("tgt"),
        P("src", "tgt", None),
        P("src", "tgt", None),
        P("src", "tgt"),
    )
    return jax.shard_map(
        local, mesh=mesh, in_specs=placed, out_specs=(P("src"), P("tgt")), check_vma=False
    )
```

```python
import functools

import jax
import jax.numpy as jnp
from jax import lax
from jax.experimental import pallas as pl
from jax.experimental.pallas import tpu as pltpu
from jax.sharding import PartitionSpec as P

BLK = 2048
TB_DEV = 8
LANES = 128
DEPTH = 128
CHUNK = 256
LOG2E = 1.4426950408889634
LN2 = 0.6931471805599453
EMPTY = -1e30
MARGIN = 60.0
ROW_LIMIT = 2.0**120
UP = 100.0
COL_LIMIT = 2.0**-90
F32 = jnp.float32
BF16 = jnp.bfloat16


def split3(x):
    high = x.astype(BF16)
    rest = x - high.astype(F32)
    mid = rest.astype(BF16)
    low = rest - mid.astype(F32)
    return high.astype(F32), mid.astype(F32), low


def stacked(pieces):
    row = lax.broadcasted_iota(jnp.int32, (16, BLK), 0)
    out = jnp.zeros((16, BLK), F32)
    for index, piece in enumerate(pieces):
        out = jnp.where(row == index, piece, out)
    return out.astype(BF16)


def block(index):
    return pl.ds(pl.multiple_of(index * BLK, BLK), BLK)


def weight_of(level):
    return jnp.where(
        level == 0, 0.125, jnp.where(level == 1, 0.25, jnp.where(level == 2, 0.5, 1.0))
    ).astype(F32)


def prep_tgt(tgt_ref, pot_ref, rep_ref, index):
    raw = tgt_ref[:, block(index)]
    cells = raw.astype(F32)
    norm = jnp.sum(cells * cells, axis=0, keepdims=True)
    extra = stacked(
        [*split3(-LOG2E * norm), *split3(LOG2E * pot_ref[:, block(index)]), 1.0, 1.0, 1.0]
    )
    full = jnp.concatenate([raw, raw, raw, extra, jnp.zeros((16, BLK), BF16)], axis=0)
    rep_ref[...] = full.T


def prep_src(src_ref, rhs_ref, index, weight):
    cells = src_ref[:, block(index)].astype(F32)
    norm = jnp.sum(cells * cells, axis=0, keepdims=True)
    high, mid, low = split3(cells * (2.0 * LOG2E * weight))
    rhs_ref[0:32, :] = high.astype(BF16)
    rhs_ref[32:64, :] = mid.astype(BF16)
    rhs_ref[64:96, :] = low.astype(BF16)
    return (LOG2E * weight) * norm


def set_extra(rhs_ref, weight, term):
    rhs_ref[96:112, :] = stacked([weight, weight, weight, 1.0, 1.0, 1.0, *split3(term)])


def scores(rep_ref, rhs_ref, row, col):
    return jnp.dot(
        rep_ref[pl.ds(row, CHUNK), :],
        rhs_ref[:, col : col + CHUNK],
        preferred_element_type=F32,
    )


def log_add(first, second):
    peak = jnp.maximum(first, second)
    return peak + jnp.log2(jnp.exp2(first - peak) + jnp.exp2(second - peak))


def for_tiles(count, prep, main, even, odd):
    def pair(step, carry):
        prep(2 * step + 1, odd)
        main(2 * step, even)

        @pl.when(2 * step + 1 < count)
        def _():
            prep(2 * step + 2, even)
            main(2 * step + 1, odd)

        return carry

    prep(0, even)
    lax.fori_loop(0, (count + 1) // 2, pair, 0)


def row_kernel(
    ids,
    levels,
    counts,
    cores,
    tgt_ref,
    pot_ref,
    src_ref,
    kept_ref,
    sent_ref,
    lse_ref,
    top_ref,
    *operands,
):
    count = counts[0]
    for rhs_ref in (operands[1], operands[4]):
        rhs_ref[112:128, :] = jnp.zeros((16, BLK), BF16)

    def prep(slot, refs):
        rep_ref, rhs_ref, base_ref = refs
        slot = jnp.minimum(slot, count - 1)
        weight = weight_of(levels[slot])
        prep_tgt(tgt_ref, pot_ref, rep_ref, ids[slot] % TB_DEV)
        norm = prep_src(src_ref, rhs_ref, ids[slot] // TB_DEV, weight)
        set_extra(rhs_ref, weight, jnp.zeros((1, BLK), F32))
        mean = jnp.dot(jnp.ones((16, BLK), BF16), rep_ref[...], preferred_element_type=F32)
        mean = (mean * (1.0 / BLK)).astype(BF16)
        shift = MARGIN + jnp.dot(mean, rhs_ref[...], preferred_element_type=F32)[0:1]
        set_extra(rhs_ref, weight, -shift)
        base_ref[...] = shift - norm

    def merge(slot, col, value):
        cols = pl.ds(pl.multiple_of(ids[slot] // TB_DEV * BLK + col, CHUNK), CHUNK)
        lse_ref[:, cols] = log_add(lse_ref[:, cols], value)

    def main(slot, refs):
        rep_ref, rhs_ref, base_ref = refs
        for col in range(0, BLK, CHUNK):
            total = jnp.zeros((8, CHUNK), F32)
            for row in range(0, BLK, CHUNK):
                part = jnp.exp2(scores(rep_ref, rhs_ref, row, col))
                total = total + jnp.sum(part.reshape(CHUNK // 8, 8, CHUNK), axis=0)
            total = jnp.sum(total, axis=0, keepdims=True)
            cols = slice(col, col + CHUNK)
            top_ref[:, cols] = jnp.maximum(top_ref[:, cols], total)
            merge(slot, col, base_ref[:, cols] + jnp.log2(total))

    def safe_tile(slot, carry):
        rep_ref, rhs_ref, base_ref = operands[:3]
        prep(slot, operands[:3])
        weight = weight_of(levels[slot])
        norm = prep_src(src_ref, rhs_ref, ids[slot] // TB_DEV, weight)
        set_extra(rhs_ref, weight, jnp.zeros((1, BLK), F32))
        for col in range(0, BLK, CHUNK):

            def peak_part(step, peak):
                row = pl.multiple_of(step * CHUNK, CHUNK)
                part = scores(rep_ref, rhs_ref, row, col)
                return jnp.maximum(peak, jnp.max(part.reshape(CHUNK // 8, 8, CHUNK), axis=0))

            peak = lax.fori_loop(0, BLK // CHUNK, peak_part, jnp.full((8, CHUNK), EMPTY, F32))
            peak = jnp.max(peak, axis=0, keepdims=True)

            def sum_part(step, total):
                row = pl.multiple_of(step * CHUNK, CHUNK)
                part = jnp.exp2(scores(rep_ref, rhs_ref, row, col) - peak)
                return total + jnp.sum(part.reshape(CHUNK // 8, 8, CHUNK), axis=0)

            total = lax.fori_loop(0, BLK // CHUNK, sum_part, jnp.zeros((8, CHUNK), F32))
            total = jnp.sum(total, axis=0, keepdims=True)
            merge(slot, col, peak - norm[:, col : col + CHUNK] + jnp.log2(total))
        return carry

    lse_ref[...] = jnp.full(lse_ref.shape, EMPTY, F32)
    top_ref[...] = jnp.zeros(top_ref.shape, F32)
    for_tiles(count, prep, main, operands[:3], operands[3:])

    @pl.when(jnp.logical_not(jnp.max(top_ref[...]) < ROW_LIMIT))
    def _():
        lse_ref[...] = jnp.full(lse_ref.shape, EMPTY, F32)
        lax.fori_loop(0, count, safe_tile, 0)

    half = kept_ref.shape[1]
    kept_ref[...] = lse_ref[:, pl.ds(pl.multiple_of(cores[0] * half, half), half)]
    sent_ref[...] = lse_ref[:, pl.ds(pl.multiple_of((1 - cores[0]) * half, half), half)]


def col_kernel(
    ids,
    levels,
    counts,
    cores,
    tgt_ref,
    pot_ref,
    src_ref,
    own_ref,
    other_ref,
    lse_ref,
    wide_ref,
    *operands,
):
    count = counts[0]
    half_blocks = own_ref.shape[1] // BLK
    for rhs_ref in (operands[1], operands[3]):
        rhs_ref[112:128, :] = jnp.zeros((16, BLK), BF16)

    def prep(slot, refs):
        rep_ref, rhs_ref = refs
        slot = jnp.minimum(slot, count - 1)
        src_block = ids[slot] // TB_DEV
        weight = weight_of(levels[slot])
        prep_tgt(tgt_ref, pot_ref, rep_ref, ids[slot] % TB_DEV)
        norm = prep_src(src_ref, rhs_ref, src_block, weight)
        cols = block(src_block % half_blocks)
        potential = jnp.where(
            src_block // half_blocks == cores[0], own_ref[:, cols], other_ref[:, cols]
        )
        set_extra(rhs_ref, weight, potential - norm + (UP - LOG2E))

    def main(slot, refs):
        rep_ref, rhs_ref = refs
        start = ids[slot] % TB_DEV * BLK
        for row in range(0, BLK, CHUNK):
            total = jnp.zeros((CHUNK, LANES), F32)
            for col in range(0, BLK, CHUNK):
                part = jnp.exp2(scores(rep_ref, rhs_ref, row, col))
                for lane in range(0, CHUNK, LANES):
                    total = total + part[:, lane : lane + LANES]
            cols = pl.ds(pl.multiple_of(start + row, CHUNK), CHUNK)
            lse_ref[:, cols] = lse_ref[:, cols] + jnp.sum(total.T, axis=0, keepdims=True)

    def safe_tile(slot, carry):
        rep_ref, rhs_ref = operands[:2]
        prep(slot, operands[:2])
        start = ids[slot] % TB_DEV * BLK

        def step(index, inner):
            row = pl.multiple_of(index * CHUNK, CHUNK)
            peak = jnp.full((CHUNK, LANES), EMPTY, F32)
            for col in range(0, BLK, CHUNK):
                part = scores(rep_ref, rhs_ref, row, col)
                for lane in range(0, CHUNK, LANES):
                    peak = jnp.maximum(peak, part[:, lane : lane + LANES])
            total = jnp.zeros((CHUNK, LANES), F32)
            for col in range(0, BLK, CHUNK):
                part = scores(rep_ref, rhs_ref, row, col)
                for lane in range(0, CHUNK, LANES):
                    total = total + jnp.exp2(part[:, lane : lane + LANES] - peak)
            rows = pl.ds(pl.multiple_of(start + row, CHUNK), CHUNK)
            wide_ref[rows, :] = log_add(wide_ref[rows, :], peak + jnp.log2(total))
            return inner

        lax.fori_loop(0, BLK // CHUNK, step, 0)
        return carry

    def lowest(slot, low):
        return jnp.minimum(low, lse_ref[:, block(ids[slot] % TB_DEV)])

    lse_ref[...] = jnp.zeros(lse_ref.shape, F32)
    for_tiles(count, prep, main, operands[:2], operands[2:])
    low = lax.fori_loop(0, count, lowest, jnp.full((1, BLK), 1.0, F32))
    sums = lse_ref[...]
    lse_ref[...] = jnp.where(sums > 0.0, jnp.log2(sums), EMPTY)

    @pl.when(jnp.logical_not(jnp.min(low) >= COL_LIMIT))
    def _():
        wide_ref[...] = jnp.full(wide_ref.shape, EMPTY, F32)
        lax.fori_loop(0, count, safe_tile, 0)

        def narrow(index, inner):
            cols = pl.ds(pl.multiple_of(index * CHUNK, CHUNK), CHUNK)
            wide = wide_ref[cols, :].T
            peak = jnp.max(wide, axis=0, keepdims=True)
            lse_ref[:, cols] = peak + jnp.log2(
                jnp.sum(jnp.exp2(wide - peak), axis=0, keepdims=True)
            )
            return inner

        lax.fori_loop(0, wide_ref.shape[0] // CHUNK, narrow, 0)


WHOLE = pl.BlockSpec(memory_space=pltpu.VMEM)
SCALAR = pl.BlockSpec(memory_space=pltpu.SMEM)
PARAMS = pltpu.CompilerParams(vmem_limit_bytes=24 * 2**20)
TGT_OPERAND = pltpu.VMEM((BLK, DEPTH), BF16)
SRC_OPERAND = pltpu.VMEM((DEPTH, BLK), BF16)
ROW = pltpu.VMEM((1, BLK), F32)


def row_pass(scalars, tgt, pot, src):
    half = jax.ShapeDtypeStruct((1, src.shape[1] // 2), F32)
    return pl.pallas_call(
        row_kernel,
        out_shape=(half, half),
        in_specs=[SCALAR] * 4 + [WHOLE] * 3,
        out_specs=(WHOLE, WHOLE),
        scratch_shapes=[pltpu.VMEM((1, src.shape[1]), F32), ROW]
        + [TGT_OPERAND, SRC_OPERAND, ROW] * 2,
        compiler_params=PARAMS,
        name="row_pass",
    )(*scalars, tgt, pot, src)


def col_pass(scalars, tgt, pot, src, own, other):
    return pl.pallas_call(
        col_kernel,
        out_shape=jax.ShapeDtypeStruct((1, tgt.shape[1]), F32),
        in_specs=[SCALAR] * 4 + [WHOLE] * 5,
        out_specs=WHOLE,
        scratch_shapes=[pltpu.VMEM((tgt.shape[1], LANES), F32)]
        + [TGT_OPERAND, SRC_OPERAND] * 2,
        compiler_params=PARAMS,
        name="col_pass",
    )(*scalars, tgt, pot, src, own, other)


def log_sum(parts):
    peak = functools.reduce(jnp.maximum, parts)
    return peak + jnp.log2(sum(jnp.exp2(part - peak) for part in parts))


def exchanged(value, axis, masks):
    size = lax.axis_size(axis)
    parts = [
        lax.ppermute(value, axis, [(i, i ^ mask) for i in range(size)]) for mask in masks
    ]
    return log_sum([value, *parts])


def local(src, tgt, pot, src_log, tgt_log, tile_ids, tile_level, tile_count):
    core = lax.axis_index("tgt") % 2
    scalars = (tile_ids[0, 0], tile_level[0, 0], tile_count[0], core[None])
    src_t, tgt_t = src.T, tgt.T
    kept, sent = row_pass(scalars, tgt_t, pot[None], src_t)

    swap = [(i, i ^ 1) for i in range(lax.axis_size("tgt"))]
    half = log_sum([kept[0], lax.ppermute(sent[0], "tgt", swap)])
    half = exchanged(half, "tgt", (2, 4, 6))
    half = exchanged(half, "tgt", (8, 16, 24))
    src_half = lax.dynamic_index_in_dim(src_log.reshape(2, -1), core, 0, False)
    own = LOG2E * src_half - half
    other = lax.ppermute(own, "tgt", swap)

    col_lse = col_pass(scalars, tgt_t, pot[None], src_t, own[None], other[None])[0]
    col_lse = exchanged(col_lse, "src", (1, 2, 3))
    col_lse = exchanged(col_lse, "src", (7,))
    new_pot = tgt_log + pot - (LN2 * (col_lse - UP) + 1.0)
    sp = jnp.where(core == 0, jnp.concatenate([own, other]), jnp.concatenate([other, own]))
    return LN2 * sp, new_pot


def solution(mesh):
    placed = (
        P("src", None),
        P("tgt", None),
        P("tgt"),
        P("src"),
        P("tgt"),
        P("src", "tgt", None),
        P("src", "tgt", None),
        P("src", "tgt"),
    )
    return jax.shard_map(
        local, mesh=mesh, in_specs=placed, out_specs=(P("src"), P("tgt")), check_vma=False
    )
```

```python
import functools

import jax
import jax.numpy as jnp
from jax import lax
from jax.experimental import pallas as pl
from jax.experimental.pallas import tpu as pltpu
from jax.sharding import PartitionSpec as P

BLK = 2048
TB_DEV = 8
LANES = 128
DEPTH = 128
CHUNK = 256
LOG2E = 1.4426950408889634
LN2 = 0.6931471805599453
EMPTY = -1e30
MARGIN = 60.0
ROW_LIMIT = 2.0**120
UP = 100.0
COL_LIMIT = 2.0**-90
F32 = jnp.float32
BF16 = jnp.bfloat16


def split3(x):
    high = x.astype(BF16)
    rest = x - high.astype(F32)
    mid = rest.astype(BF16)
    low = rest - mid.astype(F32)
    return high.astype(F32), mid.astype(F32), low


def stacked(pieces):
    row = lax.broadcasted_iota(jnp.int32, (16, BLK), 0)
    out = jnp.zeros((16, BLK), F32)
    for index, piece in enumerate(pieces):
        out = jnp.where(row == index, piece, out)
    return out.astype(BF16)


def block(index):
    return pl.ds(pl.multiple_of(index * BLK, BLK), BLK)


def weight_of(level):
    return jnp.where(
        level == 0, 0.125, jnp.where(level == 1, 0.25, jnp.where(level == 2, 0.5, 1.0))
    ).astype(F32)


def prep_tgt(raw, potential, rep_ref):
    cells = raw.astype(F32)
    norm = jnp.sum(cells * cells, axis=0, keepdims=True)
    extra = stacked(
        [*split3(-LOG2E * norm), *split3(LOG2E * potential), 1.0, 1.0, 1.0]
    )
    full = jnp.concatenate([raw, raw, raw, extra, jnp.zeros((16, BLK), BF16)], axis=0)
    rep_ref[...] = full.T
    return cells, norm


def prep_src(raw, rhs_ref, weight):
    cells = raw.astype(F32)
    norm = jnp.sum(cells * cells, axis=0, keepdims=True)
    scaled = cells * (2.0 * LOG2E * weight)
    high, mid, low = split3(scaled)
    rhs_ref[0:32, :] = high.astype(BF16)
    rhs_ref[32:64, :] = mid.astype(BF16)
    rhs_ref[64:96, :] = low.astype(BF16)
    return scaled, (LOG2E * weight) * norm


def set_extra(rhs_ref, weight, term):
    rhs_ref[96:112, :] = stacked([weight, weight, weight, 1.0, 1.0, 1.0, *split3(term)])


def scores(rep_ref, rhs_ref, row, col):
    return jnp.dot(
        rep_ref[pl.ds(row, CHUNK), :],
        rhs_ref[:, col : col + CHUNK],
        preferred_element_type=F32,
    )


def log_add(first, second):
    peak = jnp.maximum(first, second)
    return peak + jnp.log2(jnp.exp2(first - peak) + jnp.exp2(second - peak))


def for_tiles(count, prep, main, even, odd):
    def pair(step, carry):
        prep(2 * step + 1, odd)
        main(2 * step, even)

        @pl.when(2 * step + 1 < count)
        def _():
            prep(2 * step + 2, even)
            main(2 * step + 1, odd)

        return carry

    prep(0, even)
    lax.fori_loop(0, (count + 1) // 2, pair, 0)


def row_kernel(
    cores,
    ids_hbm,
    levels_hbm,
    counts_hbm,
    tgt_hbm,
    pot_hbm,
    src_hbm,
    kept_ref,
    sent_ref,
    ids,
    levels,
    counts,
    list_sems,
    tgt_ref,
    pot_ref,
    src_ref,
    sems,
    lse_ref,
    top_ref,
    *operands,
):
    lists = [
        pltpu.make_async_copy(source, target, list_sems.at[index])
        for index, (source, target) in enumerate(
            [(counts_hbm, counts), (ids_hbm, ids), (levels_hbm, levels)]
        )
    ]
    for copy in lists:
        copy.start()
    for rhs_ref in (operands[1], operands[4]):
        rhs_ref[112:128, :] = jnp.zeros((16, BLK), BF16)
    lse_ref[...] = jnp.full(lse_ref.shape, EMPTY, F32)
    top_ref[...] = jnp.zeros(top_ref.shape, F32)
    for copy in lists:
        copy.wait()
    count = counts[0]

    def fetches(slot):
        src_cols, tgt_cols = block(ids[slot] // TB_DEV), block(ids[slot] % TB_DEV)
        return [
            pltpu.make_async_copy(tgt_hbm.at[:, tgt_cols], tgt_ref.at[slot], sems.at[0, slot]),
            pltpu.make_async_copy(src_hbm.at[:, src_cols], src_ref.at[slot], sems.at[1, slot]),
            pltpu.make_async_copy(pot_hbm.at[:, tgt_cols], pot_ref.at[slot], sems.at[2, slot]),
        ]

    def fetch(slot, carry):
        for copy in fetches(slot):
            copy.start()
        return carry

    lax.fori_loop(0, count, fetch, 0)

    def prep(slot, refs, wait=True):
        rep_ref, rhs_ref, base_ref = refs
        if wait:

            @pl.when(slot < count)
            def _():
                for copy in fetches(slot):
                    copy.wait()

        slot = jnp.minimum(slot, count - 1)
        weight = weight_of(levels[slot])
        cells, tgt_norm = prep_tgt(tgt_ref[slot], pot_ref[slot], rep_ref)
        scaled, norm = prep_src(src_ref[slot], rhs_ref, weight)
        offset = LOG2E * (pot_ref[slot] - weight * tgt_norm)
        centre = jnp.sum(cells, axis=1, keepdims=True) * (1.0 / BLK)
        level = MARGIN + jnp.sum(offset, axis=1, keepdims=True) * (1.0 / BLK)
        shift = level + jnp.sum(scaled * centre, axis=0, keepdims=True)
        set_extra(rhs_ref, weight, -shift)
        base_ref[...] = shift - norm

    def merge(slot, col, value):
        cols = pl.ds(pl.multiple_of(ids[slot] // TB_DEV * BLK + col, CHUNK), CHUNK)
        lse_ref[:, cols] = log_add(lse_ref[:, cols], value)

    def main(slot, refs):
        rep_ref, rhs_ref, base_ref = refs
        for col in range(0, BLK, CHUNK):
            total = jnp.zeros((8, CHUNK), F32)
            for row in range(0, BLK, CHUNK):
                part = jnp.exp2(scores(rep_ref, rhs_ref, row, col))
                total = total + jnp.sum(part.reshape(CHUNK // 8, 8, CHUNK), axis=0)
            total = jnp.sum(total, axis=0, keepdims=True)
            cols = slice(col, col + CHUNK)
            top_ref[:, cols] = jnp.maximum(top_ref[:, cols], total)
            merge(slot, col, base_ref[:, cols] + jnp.log2(total))

    def safe_tile(slot, carry):
        rep_ref, rhs_ref, base_ref = operands[:3]
        prep(slot, operands[:3], False)
        weight = weight_of(levels[slot])
        _, norm = prep_src(src_ref[slot], rhs_ref, weight)
        set_extra(rhs_ref, weight, jnp.zeros((1, BLK), F32))
        for col in range(0, BLK, CHUNK):

            def peak_part(step, peak):
                row = pl.multiple_of(step * CHUNK, CHUNK)
                part = scores(rep_ref, rhs_ref, row, col)
                return jnp.maximum(peak, jnp.max(part.reshape(CHUNK // 8, 8, CHUNK), axis=0))

            peak = lax.fori_loop(0, BLK // CHUNK, peak_part, jnp.full((8, CHUNK), EMPTY, F32))
            peak = jnp.max(peak, axis=0, keepdims=True)

            def sum_part(step, total):
                row = pl.multiple_of(step * CHUNK, CHUNK)
                part = jnp.exp2(scores(rep_ref, rhs_ref, row, col) - peak)
                return total + jnp.sum(part.reshape(CHUNK // 8, 8, CHUNK), axis=0)

            total = lax.fori_loop(0, BLK // CHUNK, sum_part, jnp.zeros((8, CHUNK), F32))
            total = jnp.sum(total, axis=0, keepdims=True)
            merge(slot, col, peak - norm[:, col : col + CHUNK] + jnp.log2(total))
        return carry

    for_tiles(count, prep, main, operands[:3], operands[3:])

    @pl.when(jnp.logical_not(jnp.max(top_ref[...]) < ROW_LIMIT))
    def _():
        lse_ref[...] = jnp.full(lse_ref.shape, EMPTY, F32)
        lax.fori_loop(0, count, safe_tile, 0)

    half = kept_ref.shape[1]
    kept_ref[...] = lse_ref[:, pl.ds(pl.multiple_of(cores[0] * half, half), half)]
    sent_ref[...] = lse_ref[:, pl.ds(pl.multiple_of((1 - cores[0]) * half, half), half)]


def col_kernel(
    ids,
    levels,
    counts,
    cores,
    tgt_ref,
    pot_ref,
    src_ref,
    own_ref,
    other_ref,
    lse_ref,
    wide_ref,
    *operands,
):
    count = counts[0]
    half_blocks = own_ref.shape[1] // BLK
    for rhs_ref in (operands[1], operands[3]):
        rhs_ref[112:128, :] = jnp.zeros((16, BLK), BF16)

    def prep(slot, refs):
        rep_ref, rhs_ref = refs
        slot = jnp.minimum(slot, count - 1)
        src_block = ids[slot] // TB_DEV
        weight = weight_of(levels[slot])
        tgt_cols = block(ids[slot] % TB_DEV)
        prep_tgt(tgt_ref[:, tgt_cols], pot_ref[:, tgt_cols], rep_ref)
        _, norm = prep_src(src_ref[:, block(src_block)], rhs_ref, weight)
        cols = block(src_block % half_blocks)
        potential = jnp.where(
            src_block // half_blocks == cores[0], own_ref[:, cols], other_ref[:, cols]
        )
        set_extra(rhs_ref, weight, potential - norm + (UP - LOG2E))

    def main(slot, refs):
        rep_ref, rhs_ref = refs
        start = ids[slot] % TB_DEV * BLK
        for row in range(0, BLK, CHUNK):
            total = jnp.zeros((CHUNK, LANES), F32)
            for col in range(0, BLK, CHUNK):
                part = jnp.exp2(scores(rep_ref, rhs_ref, row, col))
                for lane in range(0, CHUNK, LANES):
                    total = total + part[:, lane : lane + LANES]
            cols = pl.ds(pl.multiple_of(start + row, CHUNK), CHUNK)
            lse_ref[:, cols] = lse_ref[:, cols] + jnp.sum(total.T, axis=0, keepdims=True)

    def safe_tile(slot, carry):
        rep_ref, rhs_ref = operands[:2]
        prep(slot, operands[:2])
        start = ids[slot] % TB_DEV * BLK

        def step(index, inner):
            row = pl.multiple_of(index * CHUNK, CHUNK)
            peak = jnp.full((CHUNK, LANES), EMPTY, F32)
            for col in range(0, BLK, CHUNK):
                part = scores(rep_ref, rhs_ref, row, col)
                for lane in range(0, CHUNK, LANES):
                    peak = jnp.maximum(peak, part[:, lane : lane + LANES])
            total = jnp.zeros((CHUNK, LANES), F32)
            for col in range(0, BLK, CHUNK):
                part = scores(rep_ref, rhs_ref, row, col)
                for lane in range(0, CHUNK, LANES):
                    total = total + jnp.exp2(part[:, lane : lane + LANES] - peak)
            rows = pl.ds(pl.multiple_of(start + row, CHUNK), CHUNK)
            wide_ref[rows, :] = log_add(wide_ref[rows, :], peak + jnp.log2(total))
            return inner

        lax.fori_loop(0, BLK // CHUNK, step, 0)
        return carry

    def lowest(slot, low):
        return jnp.minimum(low, lse_ref[:, block(ids[slot] % TB_DEV)])

    lse_ref[...] = jnp.zeros(lse_ref.shape, F32)
    for_tiles(count, prep, main, operands[:2], operands[2:])
    low = lax.fori_loop(0, count, lowest, jnp.full((1, BLK), 1.0, F32))
    sums = lse_ref[...]
    lse_ref[...] = jnp.where(sums > 0.0, jnp.log2(sums), EMPTY)

    @pl.when(jnp.logical_not(jnp.min(low) >= COL_LIMIT))
    def _():
        wide_ref[...] = jnp.full(wide_ref.shape, EMPTY, F32)
        lax.fori_loop(0, count, safe_tile, 0)

        def narrow(index, inner):
            cols = pl.ds(pl.multiple_of(index * CHUNK, CHUNK), CHUNK)
            wide = wide_ref[cols, :].T
            peak = jnp.max(wide, axis=0, keepdims=True)
            lse_ref[:, cols] = peak + jnp.log2(
                jnp.sum(jnp.exp2(wide - peak), axis=0, keepdims=True)
            )
            return inner

        lax.fori_loop(0, wide_ref.shape[0] // CHUNK, narrow, 0)


WHOLE = pl.BlockSpec(memory_space=pltpu.VMEM)
SCALAR = pl.BlockSpec(memory_space=pltpu.SMEM)
PARAMS = pltpu.CompilerParams(vmem_limit_bytes=24 * 2**20)
ROW_PARAMS = pltpu.CompilerParams(vmem_limit_bytes=60 * 2**20)
TGT_OPERAND = pltpu.VMEM((BLK, DEPTH), BF16)
SRC_OPERAND = pltpu.VMEM((DEPTH, BLK), BF16)
ROW = pltpu.VMEM((1, BLK), F32)


def row_pass(scalars, tgt, pot, src):
    half = jax.ShapeDtypeStruct((1, src.shape[1] // 2), F32)
    ids, levels, counts, cores = scalars
    slots = ids.shape[0]
    return pl.pallas_call(
        row_kernel,
        out_shape=(half, half),
        in_specs=[SCALAR] + [pl.BlockSpec(memory_space=pltpu.HBM)] * 6,
        out_specs=(WHOLE, WHOLE),
        scratch_shapes=[
            pltpu.SMEM(ids.shape, jnp.int32),
            pltpu.SMEM(levels.shape, jnp.int32),
            pltpu.SMEM(counts.shape, jnp.int32),
            pltpu.SemaphoreType.DMA((3,)),
            pltpu.VMEM((slots, tgt.shape[0], BLK), BF16),
            pltpu.VMEM((slots, 1, BLK), F32),
            pltpu.VMEM((slots, src.shape[0], BLK), BF16),
            pltpu.SemaphoreType.DMA((3, slots)),
            pltpu.VMEM((1, src.shape[1]), F32),
            ROW,
        ]
        + [TGT_OPERAND, SRC_OPERAND, ROW] * 2,
        compiler_params=ROW_PARAMS,
        name="row_pass",
    )(cores, ids, levels, counts, tgt, pot, src)


def col_pass(scalars, tgt, pot, src, own, other):
    return pl.pallas_call(
        col_kernel,
        out_shape=jax.ShapeDtypeStruct((1, tgt.shape[1]), F32),
        in_specs=[SCALAR] * 4 + [WHOLE] * 5,
        out_specs=WHOLE,
        scratch_shapes=[pltpu.VMEM((tgt.shape[1], LANES), F32)]
        + [TGT_OPERAND, SRC_OPERAND] * 2,
        compiler_params=PARAMS,
        name="col_pass",
    )(*scalars, tgt, pot, src, own, other)


def log_sum(parts):
    peak = functools.reduce(jnp.maximum, parts)
    return peak + jnp.log2(sum(jnp.exp2(part - peak) for part in parts))


def exchanged(value, axis, masks):
    size = lax.axis_size(axis)
    parts = [
        lax.ppermute(value, axis, [(i, i ^ mask) for i in range(size)]) for mask in masks
    ]
    return log_sum([value, *parts])


def local(src, tgt, pot, src_log, tgt_log, tile_ids, tile_level, tile_count):
    core = lax.axis_index("tgt") % 2
    scalars = (tile_ids[0, 0], tile_level[0, 0], tile_count[0], core[None])
    src_t, tgt_t = src.T, tgt.T
    kept, sent = row_pass(scalars, tgt_t, pot[None], src_t)

    swap = [(i, i ^ 1) for i in range(lax.axis_size("tgt"))]
    half = log_sum([kept[0], lax.ppermute(sent[0], "tgt", swap)])
    half = exchanged(half, "tgt", (2, 4, 6))
    half = exchanged(half, "tgt", (8, 16, 24))
    src_half = lax.dynamic_index_in_dim(src_log.reshape(2, -1), core, 0, False)
    own = LOG2E * src_half - half
    other = lax.ppermute(own, "tgt", swap)

    col_lse = col_pass(scalars, tgt_t, pot[None], src_t, own[None], other[None])[0]
    col_lse = exchanged(col_lse, "src", (1, 6, 7))
    col_lse = exchanged(col_lse, "src", (2,))
    new_pot = tgt_log + pot - (LN2 * (col_lse - UP) + 1.0)
    sp = jnp.where(core == 0, jnp.concatenate([own, other]), jnp.concatenate([other, own]))
    return LN2 * sp, new_pot


def solution(mesh):
    placed = (
        P("src", None),
        P("tgt", None),
        P("tgt"),
        P("src"),
        P("tgt"),
        P("src", "tgt", None),
        P("src", "tgt", None),
        P("src", "tgt"),
    )
    return jax.shard_map(
        local, mesh=mesh, in_specs=placed, out_specs=(P("src"), P("tgt")), check_vma=False
    )
```

```python
import functools

import jax
import jax.numpy as jnp
from jax import lax
from jax.experimental import pallas as pl
from jax.experimental.pallas import tpu as pltpu
from jax.sharding import PartitionSpec as P

BLK = 2048
TB_DEV = 8
LANES = 128
DEPTH = 128
CHUNK = 256
LOG2E = 1.4426950408889634
LN2 = 0.6931471805599453
EMPTY = -1e30
MARGIN = 60.0
ROW_LIMIT = 2.0**120
UP = 100.0
COL_LIMIT = 2.0**-90
F32 = jnp.float32
BF16 = jnp.bfloat16


def split3(x):
    high = x.astype(BF16)
    rest = x - high.astype(F32)
    mid = rest.astype(BF16)
    low = rest - mid.astype(F32)
    return high.astype(F32), mid.astype(F32), low


def stacked(pieces):
    row = lax.broadcasted_iota(jnp.int32, (16, BLK), 0)
    out = jnp.zeros((16, BLK), F32)
    for index, piece in enumerate(pieces):
        out = jnp.where(row == index, piece, out)
    return out.astype(BF16)


def block(index):
    return pl.ds(pl.multiple_of(index * BLK, BLK), BLK)


def weight_of(level):
    return jnp.where(
        level == 0, 0.125, jnp.where(level == 1, 0.25, jnp.where(level == 2, 0.5, 1.0))
    ).astype(F32)


def prep_tgt(raw, potential, rep_ref):
    cells = raw.astype(F32)
    norm = jnp.sum(cells * cells, axis=0, keepdims=True)
    extra = stacked(
        [*split3(-LOG2E * norm), *split3(LOG2E * potential), 1.0, 1.0, 1.0]
    )
    full = jnp.concatenate([raw, raw, raw, extra, jnp.zeros((16, BLK), BF16)], axis=0)
    rep_ref[...] = full.T
    return cells, norm


def prep_src(raw, rhs_ref, weight):
    cells = raw.astype(F32)
    norm = jnp.sum(cells * cells, axis=0, keepdims=True)
    scaled = cells * (2.0 * LOG2E * weight)
    high, mid, low = split3(scaled)
    rhs_ref[0:32, :] = high.astype(BF16)
    rhs_ref[32:64, :] = mid.astype(BF16)
    rhs_ref[64:96, :] = low.astype(BF16)
    return scaled, (LOG2E * weight) * norm


def set_extra(rhs_ref, weight, term):
    rhs_ref[96:112, :] = stacked([weight, weight, weight, 1.0, 1.0, 1.0, *split3(term)])


def scores(rep_ref, rhs_ref, row, col):
    return jnp.dot(
        rep_ref[pl.ds(row, CHUNK), :],
        rhs_ref[:, col : col + CHUNK],
        preferred_element_type=F32,
    )


def log_add(first, second):
    peak = jnp.maximum(first, second)
    return peak + jnp.log2(jnp.exp2(first - peak) + jnp.exp2(second - peak))


def for_tiles(count, prep, main, even, odd):
    def pair(step, carry):
        prep(2 * step + 1, odd)
        main(2 * step, even)

        @pl.when(2 * step + 1 < count)
        def _():
            prep(2 * step + 2, even)
            main(2 * step + 1, odd)

        return carry

    prep(0, even)
    lax.fori_loop(0, (count + 1) // 2, pair, 0)


def row_kernel(
    ids_hbm,
    levels_hbm,
    counts_hbm,
    tgt_hbm,
    pot_hbm,
    src_hbm,
    kept_ref,
    sent_ref,
    ids,
    levels,
    counts,
    list_sems,
    tgt_ref,
    pot_ref,
    src_ref,
    sems,
    lse_ref,
    top_ref,
    *operands,
):
    lists = [
        pltpu.make_async_copy(source, target, list_sems.at[index])
        for index, (source, target) in enumerate(
            [(counts_hbm, counts), (ids_hbm, ids), (levels_hbm, levels)]
        )
    ]
    for copy in lists:
        copy.start()
    for rhs_ref in (operands[1], operands[4]):
        rhs_ref[112:128, :] = jnp.zeros((16, BLK), BF16)
    lse_ref[...] = jnp.full(lse_ref.shape, EMPTY, F32)
    top_ref[...] = jnp.zeros(top_ref.shape, F32)
    for copy in lists:
        copy.wait()
    count = counts[0, 0]

    def fetches(slot):
        src_cols, tgt_cols = block(ids[0, 0, slot] // TB_DEV), block(ids[0, 0, slot] % TB_DEV)
        return [
            pltpu.make_async_copy(tgt_hbm.at[:, tgt_cols], tgt_ref.at[slot], sems.at[0, slot]),
            pltpu.make_async_copy(src_hbm.at[:, src_cols], src_ref.at[slot], sems.at[1, slot]),
            pltpu.make_async_copy(pot_hbm.at[:, tgt_cols], pot_ref.at[slot], sems.at[2, slot]),
        ]

    def fetch(slot, carry):
        for copy in fetches(slot):
            copy.start()
        return carry

    lax.fori_loop(0, count, fetch, 0)

    def prep(slot, refs, wait=True):
        rep_ref, rhs_ref, base_ref = refs
        if wait:

            @pl.when(slot < count)
            def _():
                for copy in fetches(slot):
                    copy.wait()

        slot = jnp.minimum(slot, count - 1)
        weight = weight_of(levels[0, 0, slot])
        cells, tgt_norm = prep_tgt(tgt_ref[slot], pot_ref[slot], rep_ref)
        scaled, norm = prep_src(src_ref[slot], rhs_ref, weight)
        offset = LOG2E * (pot_ref[slot] - weight * tgt_norm)
        centre = jnp.sum(cells, axis=1, keepdims=True) * (1.0 / BLK)
        level = MARGIN + jnp.sum(offset, axis=1, keepdims=True) * (1.0 / BLK)
        shift = level + jnp.sum(scaled * centre, axis=0, keepdims=True)
        set_extra(rhs_ref, weight, -shift)
        base_ref[...] = shift - norm

    def merge(slot, col, value):
        cols = pl.ds(pl.multiple_of(ids[0, 0, slot] // TB_DEV * BLK + col, CHUNK), CHUNK)
        lse_ref[:, cols] = log_add(lse_ref[:, cols], value)

    def main(slot, refs):
        rep_ref, rhs_ref, base_ref = refs
        for col in range(0, BLK, CHUNK):
            total = jnp.zeros((8, CHUNK), F32)
            for row in range(0, BLK, CHUNK):
                part = jnp.exp2(scores(rep_ref, rhs_ref, row, col))
                total = total + jnp.sum(part.reshape(CHUNK // 8, 8, CHUNK), axis=0)
            total = jnp.sum(total, axis=0, keepdims=True)
            cols = slice(col, col + CHUNK)
            top_ref[:, cols] = jnp.maximum(top_ref[:, cols], total)
            merge(slot, col, base_ref[:, cols] + jnp.log2(total))

    def safe_tile(slot, carry):
        rep_ref, rhs_ref, base_ref = operands[:3]
        prep(slot, operands[:3], False)
        weight = weight_of(levels[0, 0, slot])
        _, norm = prep_src(src_ref[slot], rhs_ref, weight)
        set_extra(rhs_ref, weight, jnp.zeros((1, BLK), F32))
        for col in range(0, BLK, CHUNK):

            def peak_part(step, peak):
                row = pl.multiple_of(step * CHUNK, CHUNK)
                part = scores(rep_ref, rhs_ref, row, col)
                return jnp.maximum(peak, jnp.max(part.reshape(CHUNK // 8, 8, CHUNK), axis=0))

            peak = lax.fori_loop(0, BLK // CHUNK, peak_part, jnp.full((8, CHUNK), EMPTY, F32))
            peak = jnp.max(peak, axis=0, keepdims=True)

            def sum_part(step, total):
                row = pl.multiple_of(step * CHUNK, CHUNK)
                part = jnp.exp2(scores(rep_ref, rhs_ref, row, col) - peak)
                return total + jnp.sum(part.reshape(CHUNK // 8, 8, CHUNK), axis=0)

            total = lax.fori_loop(0, BLK // CHUNK, sum_part, jnp.zeros((8, CHUNK), F32))
            total = jnp.sum(total, axis=0, keepdims=True)
            merge(slot, col, peak - norm[:, col : col + CHUNK] + jnp.log2(total))
        return carry

    for_tiles(count, prep, main, operands[:3], operands[3:])

    @pl.when(jnp.logical_not(jnp.max(top_ref[...]) < ROW_LIMIT))
    def _():
        lse_ref[...] = jnp.full(lse_ref.shape, EMPTY, F32)
        lax.fori_loop(0, count, safe_tile, 0)

    half = kept_ref.shape[1]
    core = lax.axis_index("tgt") % 2
    kept_ref[...] = lse_ref[:, pl.ds(pl.multiple_of(core * half, half), half)]
    sent_ref[...] = lse_ref[:, pl.ds(pl.multiple_of((1 - core) * half, half), half)]


def col_kernel(
    ids,
    levels,
    counts,
    tgt_ref,
    pot_ref,
    src_ref,
    own_ref,
    other_ref,
    lse_ref,
    wide_ref,
    *operands,
):
    count = counts[0, 0]
    half_blocks = own_ref.shape[1] // BLK
    core = lax.axis_index("tgt") % 2
    for rhs_ref in (operands[1], operands[3]):
        rhs_ref[112:128, :] = jnp.zeros((16, BLK), BF16)

    def prep(slot, refs):
        rep_ref, rhs_ref = refs
        slot = jnp.minimum(slot, count - 1)
        src_block = ids[0, 0, slot] // TB_DEV
        weight = weight_of(levels[0, 0, slot])
        tgt_cols = block(ids[0, 0, slot] % TB_DEV)
        prep_tgt(tgt_ref[:, tgt_cols], pot_ref[:, tgt_cols], rep_ref)
        _, norm = prep_src(src_ref[:, block(src_block)], rhs_ref, weight)
        cols = block(src_block % half_blocks)
        potential = jnp.where(
            src_block // half_blocks == core, own_ref[:, cols], other_ref[:, cols]
        )
        set_extra(rhs_ref, weight, potential - norm + (UP - LOG2E))

    def main(slot, refs):
        rep_ref, rhs_ref = refs
        start = ids[0, 0, slot] % TB_DEV * BLK
        for row in range(0, BLK, CHUNK):
            total = jnp.zeros((CHUNK, LANES), F32)
            for col in range(0, BLK, CHUNK):
                part = jnp.exp2(scores(rep_ref, rhs_ref, row, col))
                for lane in range(0, CHUNK, LANES):
                    total = total + part[:, lane : lane + LANES]
            cols = pl.ds(pl.multiple_of(start + row, CHUNK), CHUNK)
            lse_ref[:, cols] = lse_ref[:, cols] + jnp.sum(total.T, axis=0, keepdims=True)

    def safe_tile(slot, carry):
        rep_ref, rhs_ref = operands[:2]
        prep(slot, operands[:2])
        start = ids[0, 0, slot] % TB_DEV * BLK

        def step(index, inner):
            row = pl.multiple_of(index * CHUNK, CHUNK)
            peak = jnp.full((CHUNK, LANES), EMPTY, F32)
            for col in range(0, BLK, CHUNK):
                part = scores(rep_ref, rhs_ref, row, col)
                for lane in range(0, CHUNK, LANES):
                    peak = jnp.maximum(peak, part[:, lane : lane + LANES])
            total = jnp.zeros((CHUNK, LANES), F32)
            for col in range(0, BLK, CHUNK):
                part = scores(rep_ref, rhs_ref, row, col)
                for lane in range(0, CHUNK, LANES):
                    total = total + jnp.exp2(part[:, lane : lane + LANES] - peak)
            rows = pl.ds(pl.multiple_of(start + row, CHUNK), CHUNK)
            wide_ref[rows, :] = log_add(wide_ref[rows, :], peak + jnp.log2(total))
            return inner

        lax.fori_loop(0, BLK // CHUNK, step, 0)
        return carry

    def lowest(slot, low):
        return jnp.minimum(low, lse_ref[:, block(ids[0, 0, slot] % TB_DEV)])

    lse_ref[...] = jnp.zeros(lse_ref.shape, F32)
    for_tiles(count, prep, main, operands[:2], operands[2:])
    low = lax.fori_loop(0, count, lowest, jnp.full((1, BLK), 1.0, F32))
    sums = lse_ref[...]
    lse_ref[...] = jnp.where(sums > 0.0, jnp.log2(sums), EMPTY)

    @pl.when(jnp.logical_not(jnp.min(low) >= COL_LIMIT))
    def _():
        wide_ref[...] = jnp.full(wide_ref.shape, EMPTY, F32)
        lax.fori_loop(0, count, safe_tile, 0)

        def narrow(index, inner):
            cols = pl.ds(pl.multiple_of(index * CHUNK, CHUNK), CHUNK)
            wide = wide_ref[cols, :].T
            peak = jnp.max(wide, axis=0, keepdims=True)
            lse_ref[:, cols] = peak + jnp.log2(
                jnp.sum(jnp.exp2(wide - peak), axis=0, keepdims=True)
            )
            return inner

        lax.fori_loop(0, wide_ref.shape[0] // CHUNK, narrow, 0)


WHOLE = pl.BlockSpec(memory_space=pltpu.VMEM)
SCALAR = pl.BlockSpec(memory_space=pltpu.SMEM)
PARAMS = pltpu.CompilerParams(vmem_limit_bytes=24 * 2**20)
ROW_PARAMS = pltpu.CompilerParams(vmem_limit_bytes=60 * 2**20)
TGT_OPERAND = pltpu.VMEM((BLK, DEPTH), BF16)
SRC_OPERAND = pltpu.VMEM((DEPTH, BLK), BF16)
ROW = pltpu.VMEM((1, BLK), F32)


def row_pass(scalars, tgt, pot, src):
    half = pltpu.VMEM((1, src.shape[1] // 2), F32)
    ids, levels, counts = scalars
    slots = ids.shape[2]
    return pl.pallas_call(
        row_kernel,
        out_shape=(half, half, *(jax.ShapeDtypeStruct(a.shape, a.dtype) for a in scalars)),
        in_specs=[pl.BlockSpec(memory_space=pltpu.HBM)] * 6,
        out_specs=(WHOLE, WHOLE, SCALAR, SCALAR, SCALAR),
        scratch_shapes=[
            pltpu.SemaphoreType.DMA((3,)),
            pltpu.VMEM((slots, tgt.shape[0], BLK), BF16),
            pltpu.VMEM((slots, 1, BLK), F32),
            pltpu.VMEM((slots, src.shape[0], BLK), BF16),
            pltpu.SemaphoreType.DMA((3, slots)),
            pltpu.VMEM((1, src.shape[1]), F32),
            ROW,
        ]
        + [TGT_OPERAND, SRC_OPERAND, ROW] * 2,
        compiler_params=ROW_PARAMS,
        name="row_pass",
    )(ids, levels, counts, tgt, pot, src)


def col_pass(scalars, tgt, pot, src, own, other):
    return pl.pallas_call(
        col_kernel,
        out_shape=jax.ShapeDtypeStruct((1, tgt.shape[1]), F32),
        in_specs=[SCALAR] * 3 + [WHOLE] * 5,
        out_specs=WHOLE,
        scratch_shapes=[pltpu.VMEM((tgt.shape[1], LANES), F32)]
        + [TGT_OPERAND, SRC_OPERAND] * 2,
        compiler_params=PARAMS,
        name="col_pass",
    )(*scalars, tgt, pot, src, own, other)


def log_sum(parts):
    peak = functools.reduce(jnp.maximum, parts)
    return peak + jnp.log2(sum(jnp.exp2(part - peak) for part in parts))


def exchanged(value, axis, masks):
    size = lax.axis_size(axis)
    parts = [
        lax.ppermute(value, axis, [(i, i ^ mask) for i in range(size)]) for mask in masks
    ]
    return log_sum([value, *parts])


def local(src, tgt, pot, src_log, tgt_log, tile_ids, tile_level, tile_count):
    core = lax.axis_index("tgt") % 2
    scalars = (tile_ids, tile_level, tile_count)
    src_t, tgt_t = src.T, tgt.T
    kept, sent, *scalars = row_pass(scalars, tgt_t, pot[None], src_t)

    swap = [(i, i ^ 1) for i in range(lax.axis_size("tgt"))]
    half = log_sum([kept[0], lax.ppermute(sent[0], "tgt", swap)])
    half = exchanged(half, "tgt", (2, 4, 6))
    half = exchanged(half, "tgt", (8, 16, 24))
    src_half = lax.dynamic_index_in_dim(src_log.reshape(2, -1), core, 0, False)
    own = LOG2E * src_half - half
    other = lax.ppermute(own, "tgt", swap)

    col_lse = col_pass(scalars, tgt_t, pot[None], src_t, own[None], other[None])[0]
    col_lse = exchanged(col_lse, "src", (1, 2, 3))
    col_lse = exchanged(col_lse, "src", (6,))
    new_pot = tgt_log + pot - (LN2 * (col_lse - UP) + 1.0)
    sp = jnp.where(core == 0, jnp.concatenate([own, other]), jnp.concatenate([other, own]))
    return LN2 * sp, new_pot


def solution(mesh):
    placed = (
        P("src", None),
        P("tgt", None),
        P("tgt"),
        P("src"),
        P("tgt"),
        P("src", "tgt", None),
        P("src", "tgt", None),
        P("src", "tgt"),
    )
    return jax.shard_map(
        local, mesh=mesh, in_specs=placed, out_specs=(P("src"), P("tgt")), check_vma=False
    )
```

```python
import functools

import jax
import jax.numpy as jnp
from jax import lax
from jax.experimental import pallas as pl
from jax.experimental.pallas import tpu as pltpu
from jax.sharding import PartitionSpec as P

BLK = 2048
TB_DEV = 8
LANES = 128
DEPTH = 128
CHUNK = 256
LOG2E = 1.4426950408889634
LN2 = 0.6931471805599453
EMPTY = -1e30
MARGIN = 60.0
ROW_LIMIT = 2.0**120
UP = 100.0
COL_LIMIT = 2.0**-90
F32 = jnp.float32
BF16 = jnp.bfloat16


def split3(x):
    high = x.astype(BF16)
    rest = x - high.astype(F32)
    mid = rest.astype(BF16)
    low = rest - mid.astype(F32)
    return high.astype(F32), mid.astype(F32), low


def stacked(pieces):
    row = lax.broadcasted_iota(jnp.int32, (16, BLK), 0)
    out = jnp.zeros((16, BLK), F32)
    for index, piece in enumerate(pieces):
        out = jnp.where(row == index, piece, out)
    return out.astype(BF16)


def block(index):
    return pl.ds(pl.multiple_of(index * BLK, BLK), BLK)


def weight_of(level):
    return jnp.where(
        level == 0, 0.125, jnp.where(level == 1, 0.25, jnp.where(level == 2, 0.5, 1.0))
    ).astype(F32)


def prep_tgt(raw, potential, rep_ref):
    cells = raw.astype(F32)
    norm = jnp.sum(cells * cells, axis=0, keepdims=True)
    extra = stacked(
        [*split3(-LOG2E * norm), *split3(LOG2E * potential), 1.0, 1.0, 1.0]
    )
    full = jnp.concatenate([raw, raw, raw, extra, jnp.zeros((16, BLK), BF16)], axis=0)
    rep_ref[...] = full.T
    return cells, norm


def prep_src(raw, rhs_ref, weight):
    cells = raw.astype(F32)
    norm = jnp.sum(cells * cells, axis=0, keepdims=True)
    scaled = cells * (2.0 * LOG2E * weight)
    high, mid, low = split3(scaled)
    rhs_ref[0:32, :] = high.astype(BF16)
    rhs_ref[32:64, :] = mid.astype(BF16)
    rhs_ref[64:96, :] = low.astype(BF16)
    return scaled, (LOG2E * weight) * norm


def set_extra(rhs_ref, weight, term):
    rhs_ref[96:112, :] = stacked([weight, weight, weight, 1.0, 1.0, 1.0, *split3(term)])


def scores(rep_ref, rhs_ref, row, col):
    return jnp.dot(
        rep_ref[pl.ds(row, CHUNK), :],
        rhs_ref[:, col : col + CHUNK],
        preferred_element_type=F32,
    )


def log_add(first, second):
    peak = jnp.maximum(first, second)
    return peak + jnp.log2(jnp.exp2(first - peak) + jnp.exp2(second - peak))


def for_tiles(count, prep, main, even, odd):
    def pair(step, carry):
        prep(2 * step + 1, odd)
        main(2 * step, even)

        @pl.when(2 * step + 1 < count)
        def _():
            prep(2 * step + 2, even)
            main(2 * step + 1, odd)

        return carry

    prep(0, even)
    lax.fori_loop(0, (count + 1) // 2, pair, 0)


def row_kernel(
    ids_hbm,
    levels_hbm,
    counts_hbm,
    tgt_hbm,
    pot_hbm,
    src_hbm,
    kept_ref,
    sent_ref,
    ids,
    levels,
    counts,
    list_sems,
    tgt_ref,
    pot_ref,
    src_ref,
    sems,
    lse_ref,
    top_ref,
    *operands,
):
    lists = [
        pltpu.make_async_copy(source, target, list_sems.at[index])
        for index, (source, target) in enumerate(
            [(counts_hbm, counts), (ids_hbm, ids), (levels_hbm, levels)]
        )
    ]
    for copy in lists:
        copy.start()
    for rhs_ref in (operands[1], operands[4]):
        rhs_ref[112:128, :] = jnp.zeros((16, BLK), BF16)
    lse_ref[...] = jnp.full(lse_ref.shape, EMPTY, F32)
    top_ref[...] = jnp.zeros(top_ref.shape, F32)
    for copy in lists:
        copy.wait()
    count = counts[0, 0]

    def fetches(slot):
        src_cols, tgt_cols = block(ids[0, 0, slot] // TB_DEV), block(ids[0, 0, slot] % TB_DEV)
        return [
            pltpu.make_async_copy(tgt_hbm.at[:, tgt_cols], tgt_ref.at[slot], sems.at[0, slot]),
            pltpu.make_async_copy(src_hbm.at[:, src_cols], src_ref.at[slot], sems.at[1, slot]),
            pltpu.make_async_copy(pot_hbm.at[:, tgt_cols], pot_ref.at[slot], sems.at[2, slot]),
        ]

    def fetch(slot, carry):
        for copy in fetches(slot):
            copy.start()
        return carry

    lax.fori_loop(0, count, fetch, 0)

    def prep(slot, refs, wait=True):
        rep_ref, rhs_ref, base_ref = refs
        if wait:

            @pl.when(slot < count)
            def _():
                for copy in fetches(slot):
                    copy.wait()

        slot = jnp.minimum(slot, count - 1)
        weight = weight_of(levels[0, 0, slot])
        cells, tgt_norm = prep_tgt(tgt_ref[slot], pot_ref[slot], rep_ref)
        scaled, norm = prep_src(src_ref[slot], rhs_ref, weight)
        offset = LOG2E * (pot_ref[slot] - weight * tgt_norm)
        centre = jnp.sum(cells, axis=1, keepdims=True) * (1.0 / BLK)
        level = MARGIN + jnp.sum(offset, axis=1, keepdims=True) * (1.0 / BLK)
        shift = level + jnp.sum(scaled * centre, axis=0, keepdims=True)
        set_extra(rhs_ref, weight, -shift)
        base_ref[...] = shift - norm

    def merge(slot, col, value):
        cols = pl.ds(pl.multiple_of(ids[0, 0, slot] // TB_DEV * BLK + col, CHUNK), CHUNK)
        lse_ref[:, cols] = log_add(lse_ref[:, cols], value)

    def main(slot, refs):
        rep_ref, rhs_ref, base_ref = refs
        for col in range(0, BLK, CHUNK):
            total = jnp.zeros((8, CHUNK), F32)
            for row in range(0, BLK, CHUNK):
                part = jnp.exp2(scores(rep_ref, rhs_ref, row, col))
                total = total + jnp.sum(part.reshape(CHUNK // 8, 8, CHUNK), axis=0)
            total = jnp.sum(total, axis=0, keepdims=True)
            cols = slice(col, col + CHUNK)
            top_ref[:, cols] = jnp.maximum(top_ref[:, cols], total)
            merge(slot, col, base_ref[:, cols] + jnp.log2(total))

    def safe_tile(slot, carry):
        rep_ref, rhs_ref, base_ref = operands[:3]
        prep(slot, operands[:3], False)
        weight = weight_of(levels[0, 0, slot])
        _, norm = prep_src(src_ref[slot], rhs_ref, weight)
        set_extra(rhs_ref, weight, jnp.zeros((1, BLK), F32))
        for col in range(0, BLK, CHUNK):

            def peak_part(step, peak):
                row = pl.multiple_of(step * CHUNK, CHUNK)
                part = scores(rep_ref, rhs_ref, row, col)
                return jnp.maximum(peak, jnp.max(part.reshape(CHUNK // 8, 8, CHUNK), axis=0))

            peak = lax.fori_loop(0, BLK // CHUNK, peak_part, jnp.full((8, CHUNK), EMPTY, F32))
            peak = jnp.max(peak, axis=0, keepdims=True)

            def sum_part(step, total):
                row = pl.multiple_of(step * CHUNK, CHUNK)
                part = jnp.exp2(scores(rep_ref, rhs_ref, row, col) - peak)
                return total + jnp.sum(part.reshape(CHUNK // 8, 8, CHUNK), axis=0)

            total = lax.fori_loop(0, BLK // CHUNK, sum_part, jnp.zeros((8, CHUNK), F32))
            total = jnp.sum(total, axis=0, keepdims=True)
            merge(slot, col, peak - norm[:, col : col + CHUNK] + jnp.log2(total))
        return carry

    for_tiles(count, prep, main, operands[:3], operands[3:])

    @pl.when(jnp.logical_not(jnp.max(top_ref[...]) < ROW_LIMIT))
    def _():
        lse_ref[...] = jnp.full(lse_ref.shape, EMPTY, F32)
        lax.fori_loop(0, count, safe_tile, 0)

    half = kept_ref.shape[1]
    core = lax.axis_index("tgt") % 2
    kept_ref[...] = lse_ref[:, pl.ds(pl.multiple_of(core * half, half), half)]
    sent_ref[...] = lse_ref[:, pl.ds(pl.multiple_of((1 - core) * half, half), half)]


def col_kernel(
    ids,
    levels,
    counts,
    tgt_ref,
    pot_ref,
    src_ref,
    own_ref,
    other_ref,
    lse_ref,
    wide_ref,
    *operands,
):
    count = counts[0, 0]
    half_blocks = own_ref.shape[1] // BLK
    core = lax.axis_index("tgt") % 2
    for rhs_ref in (operands[1], operands[3]):
        rhs_ref[112:128, :] = jnp.zeros((16, BLK), BF16)

    def prep(slot, refs):
        rep_ref, rhs_ref = refs
        slot = jnp.minimum(slot, count - 1)
        src_block = ids[0, 0, slot] // TB_DEV
        weight = weight_of(levels[0, 0, slot])
        tgt_cols = block(ids[0, 0, slot] % TB_DEV)
        prep_tgt(tgt_ref[:, tgt_cols], pot_ref[:, tgt_cols], rep_ref)
        _, norm = prep_src(src_ref[:, block(src_block)], rhs_ref, weight)
        cols = block(src_block % half_blocks)
        potential = jnp.where(
            src_block // half_blocks == core, own_ref[:, cols], other_ref[:, cols]
        )
        set_extra(rhs_ref, weight, potential - norm + (UP - LOG2E))

    def main(slot, refs):
        rep_ref, rhs_ref = refs
        start = ids[0, 0, slot] % TB_DEV * BLK
        for row in range(0, BLK, CHUNK):
            total = jnp.zeros((CHUNK, LANES), F32)
            for col in range(0, BLK, CHUNK):
                part = jnp.exp2(scores(rep_ref, rhs_ref, row, col))
                for lane in range(0, CHUNK, LANES):
                    total = total + part[:, lane : lane + LANES]
            cols = pl.ds(pl.multiple_of(start + row, CHUNK), CHUNK)
            lse_ref[:, cols] = lse_ref[:, cols] + jnp.sum(total.T, axis=0, keepdims=True)

    def safe_tile(slot, carry):
        rep_ref, rhs_ref = operands[:2]
        prep(slot, operands[:2])
        start = ids[0, 0, slot] % TB_DEV * BLK

        def step(index, inner):
            row = pl.multiple_of(index * CHUNK, CHUNK)
            peak = jnp.full((CHUNK, LANES), EMPTY, F32)
            for col in range(0, BLK, CHUNK):
                part = scores(rep_ref, rhs_ref, row, col)
                for lane in range(0, CHUNK, LANES):
                    peak = jnp.maximum(peak, part[:, lane : lane + LANES])
            total = jnp.zeros((CHUNK, LANES), F32)
            for col in range(0, BLK, CHUNK):
                part = scores(rep_ref, rhs_ref, row, col)
                for lane in range(0, CHUNK, LANES):
                    total = total + jnp.exp2(part[:, lane : lane + LANES] - peak)
            rows = pl.ds(pl.multiple_of(start + row, CHUNK), CHUNK)
            wide_ref[rows, :] = log_add(wide_ref[rows, :], peak + jnp.log2(total))
            return inner

        lax.fori_loop(0, BLK // CHUNK, step, 0)
        return carry

    def lowest(slot, low):
        return jnp.minimum(low, lse_ref[:, block(ids[0, 0, slot] % TB_DEV)])

    lse_ref[...] = jnp.zeros(lse_ref.shape, F32)
    for_tiles(count, prep, main, operands[:2], operands[2:])
    low = lax.fori_loop(0, count, lowest, jnp.full((1, BLK), 1.0, F32))
    sums = lse_ref[...]
    lse_ref[...] = jnp.where(sums > 0.0, jnp.log2(sums), EMPTY)

    @pl.when(jnp.logical_not(jnp.min(low) >= COL_LIMIT))
    def _():
        wide_ref[...] = jnp.full(wide_ref.shape, EMPTY, F32)
        lax.fori_loop(0, count, safe_tile, 0)

        def narrow(index, inner):
            cols = pl.ds(pl.multiple_of(index * CHUNK, CHUNK), CHUNK)
            wide = wide_ref[cols, :].T
            peak = jnp.max(wide, axis=0, keepdims=True)
            lse_ref[:, cols] = peak + jnp.log2(
                jnp.sum(jnp.exp2(wide - peak), axis=0, keepdims=True)
            )
            return inner

        lax.fori_loop(0, wide_ref.shape[0] // CHUNK, narrow, 0)


WHOLE = pl.BlockSpec(memory_space=pltpu.VMEM)
SCALAR = pl.BlockSpec(memory_space=pltpu.SMEM)
PARAMS = pltpu.CompilerParams(vmem_limit_bytes=24 * 2**20)
ROW_PARAMS = pltpu.CompilerParams(vmem_limit_bytes=56 * 2**20)
TGT_OPERAND = pltpu.VMEM((BLK, DEPTH), BF16)
SRC_OPERAND = pltpu.VMEM((DEPTH, BLK), BF16)
ROW = pltpu.VMEM((1, BLK), F32)


def row_pass(scalars, tgt, pot, src):
    half = pltpu.VMEM((1, src.shape[1] // 2), F32)
    ids, levels, counts = scalars
    slots = ids.shape[2]
    return pl.pallas_call(
        row_kernel,
        out_shape=(half, half),
        in_specs=[pl.BlockSpec(memory_space=pltpu.HBM)] * 6,
        out_specs=(WHOLE, WHOLE),
        scratch_shapes=[
            pltpu.SMEM(ids.shape, jnp.int32),
            pltpu.SMEM(levels.shape, jnp.int32),
            pltpu.SMEM(counts.shape, jnp.int32),
            pltpu.SemaphoreType.DMA((3,)),
            pltpu.VMEM((slots, tgt.shape[0], BLK), BF16),
            pltpu.VMEM((slots, 1, BLK), F32),
            pltpu.VMEM((slots, src.shape[0], BLK), BF16),
            pltpu.SemaphoreType.DMA((3, slots)),
            pltpu.VMEM((1, src.shape[1]), F32),
            ROW,
        ]
        + [TGT_OPERAND, SRC_OPERAND, ROW] * 2,
        compiler_params=ROW_PARAMS,
        name="row_pass",
    )(ids, levels, counts, tgt, pot, src)


def col_pass(scalars, tgt, pot, src, own, other):
    return pl.pallas_call(
        col_kernel,
        out_shape=jax.ShapeDtypeStruct((1, tgt.shape[1]), F32),
        in_specs=[SCALAR] * 3 + [WHOLE] * 5,
        out_specs=WHOLE,
        scratch_shapes=[pltpu.VMEM((tgt.shape[1], LANES), F32)]
        + [TGT_OPERAND, SRC_OPERAND] * 2,
        compiler_params=PARAMS,
        name="col_pass",
    )(*scalars, tgt, pot, src, own, other)


def log_sum(parts):
    peak = functools.reduce(jnp.maximum, parts)
    return peak + jnp.log2(sum(jnp.exp2(part - peak) for part in parts))


def exchanged(value, axis, masks):
    size = lax.axis_size(axis)
    parts = [
        lax.ppermute(value, axis, [(i, i ^ mask) for i in range(size)]) for mask in masks
    ]
    return log_sum([value, *parts])


def local(src, tgt, pot, src_log, tgt_log, tile_ids, tile_level, tile_count):
    core = lax.axis_index("tgt") % 2
    scalars = (tile_ids, tile_level, tile_count)
    src_t, tgt_t = src.T, tgt.T
    kept, sent = row_pass(scalars, tgt_t, pot[None], src_t)

    swap = [(i, i ^ 1) for i in range(lax.axis_size("tgt"))]
    half = log_sum([kept[0], lax.ppermute(sent[0], "tgt", swap)])
    half = exchanged(half, "tgt", (2, 4, 6))
    half = exchanged(half, "tgt", (8, 16, 24))
    src_half = lax.dynamic_index_in_dim(src_log.reshape(2, -1), core, 0, False)
    own = LOG2E * src_half - half
    other = lax.ppermute(own, "tgt", swap)

    col_lse = col_pass(scalars, tgt_t, pot[None], src_t, own[None], other[None])[0]
    col_lse = exchanged(col_lse, "src", (1, 2, 3))
    col_lse = exchanged(col_lse, "src", (6,))
    new_pot = tgt_log + pot - (LN2 * (col_lse - UP) + 1.0)
    sp = jnp.where(core == 0, jnp.concatenate([own, other]), jnp.concatenate([other, own]))
    return LN2 * sp, new_pot


def solution(mesh):
    placed = (
        P("src", None),
        P("tgt", None),
        P("tgt"),
        P("src"),
        P("tgt"),
        P("src", "tgt", None),
        P("src", "tgt", None),
        P("src", "tgt"),
    )
    return jax.shard_map(
        local, mesh=mesh, in_specs=placed, out_specs=(P("src"), P("tgt")), check_vma=False
    )
```

```python
import functools

import jax
import jax.numpy as jnp
from jax import lax
from jax.experimental import pallas as pl
from jax.experimental.pallas import tpu as pltpu
from jax.sharding import PartitionSpec as P

BLK = 2048
TB_DEV = 8
LANES = 128
DEPTH = 128
CHUNK = 256
LOG2E = 1.4426950408889634
LN2 = 0.6931471805599453
EMPTY = -1e30
MARGIN = 60.0
ROW_LIMIT = 2.0**120
UP = 100.0
COL_LIMIT = 2.0**-90
F32 = jnp.float32
BF16 = jnp.bfloat16


def split3(x):
    high = x.astype(BF16)
    rest = x - high.astype(F32)
    mid = rest.astype(BF16)
    low = rest - mid.astype(F32)
    return high.astype(F32), mid.astype(F32), low


def stacked(pieces):
    row = lax.broadcasted_iota(jnp.int32, (16, BLK), 0)
    out = jnp.zeros((16, BLK), F32)
    for index, piece in enumerate(pieces):
        out = jnp.where(row == index, piece, out)
    return out.astype(BF16)


def block(index):
    return pl.ds(pl.multiple_of(index * BLK, BLK), BLK)


def weight_of(level):
    return jnp.where(
        level == 0, 0.125, jnp.where(level == 1, 0.25, jnp.where(level == 2, 0.5, 1.0))
    ).astype(F32)


def prep_tgt(raw, potential, rep_ref):
    cells = raw.astype(F32)
    norm = jnp.sum(cells * cells, axis=0, keepdims=True)
    extra = stacked(
        [*split3(-LOG2E * norm), *split3(LOG2E * potential), 1.0, 1.0, 1.0]
    )
    full = jnp.concatenate([raw, raw, raw, extra, jnp.zeros((16, BLK), BF16)], axis=0)
    rep_ref[...] = full.T
    return cells, norm


def prep_src(raw, rhs_ref, weight):
    cells = raw.astype(F32)
    norm = jnp.sum(cells * cells, axis=0, keepdims=True)
    scaled = cells * (2.0 * LOG2E * weight)
    high, mid, low = split3(scaled)
    rhs_ref[0:32, :] = high.astype(BF16)
    rhs_ref[32:64, :] = mid.astype(BF16)
    rhs_ref[64:96, :] = low.astype(BF16)
    return scaled, (LOG2E * weight) * norm


def set_extra(rhs_ref, weight, term):
    rhs_ref[96:112, :] = stacked([weight, weight, weight, 1.0, 1.0, 1.0, *split3(term)])


def scores(rep_ref, rhs_ref, row, col):
    return jnp.dot(
        rep_ref[pl.ds(row, CHUNK), :],
        rhs_ref[:, col : col + CHUNK],
        preferred_element_type=F32,
    )


def log_add(first, second):
    peak = jnp.maximum(first, second)
    return peak + jnp.log2(jnp.exp2(first - peak) + jnp.exp2(second - peak))


def for_tiles(count, prep, main, even, odd):
    def pair(step, carry):
        prep(2 * step + 1, odd)
        main(2 * step, even)

        @pl.when(2 * step + 1 < count)
        def _():
            prep(2 * step + 2, even)
            main(2 * step + 1, odd)

        return carry

    prep(0, even)
    lax.fori_loop(0, (count + 1) // 2, pair, 0)


def row_kernel(
    ids_hbm,
    levels_hbm,
    counts_hbm,
    tgt_hbm,
    pot_hbm,
    src_hbm,
    kept_ref,
    sent_ref,
    tgt_ref,
    pot_ref,
    src_ref,
    ids,
    levels,
    counts,
    list_sems,
    sems,
    lse_ref,
    top_ref,
    *operands,
):
    lists = [
        pltpu.make_async_copy(source, target, list_sems.at[index])
        for index, (source, target) in enumerate(
            [(counts_hbm, counts), (ids_hbm, ids), (levels_hbm, levels)]
        )
    ]
    for copy in lists:
        copy.start()
    for rhs_ref in (operands[1], operands[4]):
        rhs_ref[112:128, :] = jnp.zeros((16, BLK), BF16)
    lse_ref[...] = jnp.full(lse_ref.shape, EMPTY, F32)
    top_ref[...] = jnp.zeros(top_ref.shape, F32)
    for copy in lists:
        copy.wait()
    count = counts[0, 0]

    def fetches(slot):
        src_cols, tgt_cols = block(ids[0, 0, slot] // TB_DEV), block(ids[0, 0, slot] % TB_DEV)
        return [
            pltpu.make_async_copy(tgt_hbm.at[:, tgt_cols], tgt_ref.at[slot], sems.at[0, slot]),
            pltpu.make_async_copy(src_hbm.at[:, src_cols], src_ref.at[slot], sems.at[1, slot]),
            pltpu.make_async_copy(pot_hbm.at[:, tgt_cols], pot_ref.at[slot], sems.at[2, slot]),
        ]

    def fetch(slot, carry):
        for copy in fetches(slot):
            copy.start()
        return carry

    lax.fori_loop(0, count, fetch, 0)

    def prep(slot, refs, wait=True):
        rep_ref, rhs_ref, base_ref = refs
        if wait:

            @pl.when(slot < count)
            def _():
                for copy in fetches(slot):
                    copy.wait()

        slot = jnp.minimum(slot, count - 1)
        weight = weight_of(levels[0, 0, slot])
        cells, tgt_norm = prep_tgt(tgt_ref[slot], pot_ref[slot], rep_ref)
        scaled, norm = prep_src(src_ref[slot], rhs_ref, weight)
        offset = LOG2E * (pot_ref[slot] - weight * tgt_norm)
        centre = jnp.sum(cells, axis=1, keepdims=True) * (1.0 / BLK)
        level = MARGIN + jnp.sum(offset, axis=1, keepdims=True) * (1.0 / BLK)
        shift = level + jnp.sum(scaled * centre, axis=0, keepdims=True)
        set_extra(rhs_ref, weight, -shift)
        base_ref[...] = shift - norm

    def merge(slot, col, value):
        cols = pl.ds(pl.multiple_of(ids[0, 0, slot] // TB_DEV * BLK + col, CHUNK), CHUNK)
        lse_ref[:, cols] = log_add(lse_ref[:, cols], value)

    def main(slot, refs):
        rep_ref, rhs_ref, base_ref = refs
        for col in range(0, BLK, CHUNK):
            total = jnp.zeros((8, CHUNK), F32)
            for row in range(0, BLK, CHUNK):
                part = jnp.exp2(scores(rep_ref, rhs_ref, row, col))
                total = total + jnp.sum(part.reshape(CHUNK // 8, 8, CHUNK), axis=0)
            total = jnp.sum(total, axis=0, keepdims=True)
            cols = slice(col, col + CHUNK)
            top_ref[:, cols] = jnp.maximum(top_ref[:, cols], total)
            merge(slot, col, base_ref[:, cols] + jnp.log2(total))

    def safe_tile(slot, carry):
        rep_ref, rhs_ref, base_ref = operands[:3]
        prep(slot, operands[:3], False)
        weight = weight_of(levels[0, 0, slot])
        _, norm = prep_src(src_ref[slot], rhs_ref, weight)
        set_extra(rhs_ref, weight, jnp.zeros((1, BLK), F32))
        for col in range(0, BLK, CHUNK):

            def peak_part(step, peak):
                row = pl.multiple_of(step * CHUNK, CHUNK)
                part = scores(rep_ref, rhs_ref, row, col)
                return jnp.maximum(peak, jnp.max(part.reshape(CHUNK // 8, 8, CHUNK), axis=0))

            peak = lax.fori_loop(0, BLK // CHUNK, peak_part, jnp.full((8, CHUNK), EMPTY, F32))
            peak = jnp.max(peak, axis=0, keepdims=True)

            def sum_part(step, total):
                row = pl.multiple_of(step * CHUNK, CHUNK)
                part = jnp.exp2(scores(rep_ref, rhs_ref, row, col) - peak)
                return total + jnp.sum(part.reshape(CHUNK // 8, 8, CHUNK), axis=0)

            total = lax.fori_loop(0, BLK // CHUNK, sum_part, jnp.zeros((8, CHUNK), F32))
            total = jnp.sum(total, axis=0, keepdims=True)
            merge(slot, col, peak - norm[:, col : col + CHUNK] + jnp.log2(total))
        return carry

    for_tiles(count, prep, main, operands[:3], operands[3:])

    @pl.when(jnp.logical_not(jnp.max(top_ref[...]) < ROW_LIMIT))
    def _():
        lse_ref[...] = jnp.full(lse_ref.shape, EMPTY, F32)
        lax.fori_loop(0, count, safe_tile, 0)

    half = kept_ref.shape[1]
    core = lax.axis_index("tgt") % 2
    kept_ref[...] = lse_ref[:, pl.ds(pl.multiple_of(core * half, half), half)]
    sent_ref[...] = lse_ref[:, pl.ds(pl.multiple_of((1 - core) * half, half), half)]


def col_kernel(
    ids,
    levels,
    counts,
    tgt_ref,
    pot_ref,
    src_ref,
    own_ref,
    other_ref,
    lse_ref,
    wide_ref,
    *operands,
):
    count = counts[0, 0]
    half_blocks = own_ref.shape[1] // BLK
    core = lax.axis_index("tgt") % 2
    for rhs_ref in (operands[1], operands[3]):
        rhs_ref[112:128, :] = jnp.zeros((16, BLK), BF16)

    def prep(slot, refs):
        rep_ref, rhs_ref = refs
        slot = jnp.minimum(slot, count - 1)
        src_block = ids[0, 0, slot] // TB_DEV
        weight = weight_of(levels[0, 0, slot])
        prep_tgt(tgt_ref[slot], pot_ref[slot], rep_ref)
        _, norm = prep_src(src_ref[slot], rhs_ref, weight)
        cols = block(src_block % half_blocks)
        potential = jnp.where(
            src_block // half_blocks == core, own_ref[:, cols], other_ref[:, cols]
        )
        set_extra(rhs_ref, weight, potential - norm + (UP - LOG2E))

    def main(slot, refs):
        rep_ref, rhs_ref = refs
        start = ids[0, 0, slot] % TB_DEV * BLK
        for row in range(0, BLK, CHUNK):
            total = jnp.zeros((CHUNK, LANES), F32)
            for col in range(0, BLK, CHUNK):
                part = jnp.exp2(scores(rep_ref, rhs_ref, row, col))
                for lane in range(0, CHUNK, LANES):
                    total = total + part[:, lane : lane + LANES]
            cols = pl.ds(pl.multiple_of(start + row, CHUNK), CHUNK)
            lse_ref[:, cols] = lse_ref[:, cols] + jnp.sum(total.T, axis=0, keepdims=True)

    def safe_tile(slot, carry):
        rep_ref, rhs_ref = operands[:2]
        prep(slot, operands[:2])
        start = ids[0, 0, slot] % TB_DEV * BLK

        def step(index, inner):
            row = pl.multiple_of(index * CHUNK, CHUNK)
            peak = jnp.full((CHUNK, LANES), EMPTY, F32)
            for col in range(0, BLK, CHUNK):
                part = scores(rep_ref, rhs_ref, row, col)
                for lane in range(0, CHUNK, LANES):
                    peak = jnp.maximum(peak, part[:, lane : lane + LANES])
            total = jnp.zeros((CHUNK, LANES), F32)
            for col in range(0, BLK, CHUNK):
                part = scores(rep_ref, rhs_ref, row, col)
                for lane in range(0, CHUNK, LANES):
                    total = total + jnp.exp2(part[:, lane : lane + LANES] - peak)
            rows = pl.ds(pl.multiple_of(start + row, CHUNK), CHUNK)
            wide_ref[rows, :] = log_add(wide_ref[rows, :], peak + jnp.log2(total))
            return inner

        lax.fori_loop(0, BLK // CHUNK, step, 0)
        return carry

    def lowest(slot, low):
        return jnp.minimum(low, lse_ref[:, block(ids[0, 0, slot] % TB_DEV)])

    lse_ref[...] = jnp.zeros(lse_ref.shape, F32)
    for_tiles(count, prep, main, operands[:2], operands[2:])
    low = lax.fori_loop(0, count, lowest, jnp.full((1, BLK), 1.0, F32))
    sums = lse_ref[...]
    lse_ref[...] = jnp.where(sums > 0.0, jnp.log2(sums), EMPTY)

    @pl.when(jnp.logical_not(jnp.min(low) >= COL_LIMIT))
    def _():
        wide_ref[...] = jnp.full(wide_ref.shape, EMPTY, F32)
        lax.fori_loop(0, count, safe_tile, 0)

        def narrow(index, inner):
            cols = pl.ds(pl.multiple_of(index * CHUNK, CHUNK), CHUNK)
            wide = wide_ref[cols, :].T
            peak = jnp.max(wide, axis=0, keepdims=True)
            lse_ref[:, cols] = peak + jnp.log2(
                jnp.sum(jnp.exp2(wide - peak), axis=0, keepdims=True)
            )
            return inner

        lax.fori_loop(0, wide_ref.shape[0] // CHUNK, narrow, 0)


WHOLE = pl.BlockSpec(memory_space=pltpu.VMEM)
SCALAR = pl.BlockSpec(memory_space=pltpu.SMEM)
PARAMS = pltpu.CompilerParams(vmem_limit_bytes=24 * 2**20)
ROW_PARAMS = pltpu.CompilerParams(vmem_limit_bytes=56 * 2**20)
TGT_OPERAND = pltpu.VMEM((BLK, DEPTH), BF16)
SRC_OPERAND = pltpu.VMEM((DEPTH, BLK), BF16)
ROW = pltpu.VMEM((1, BLK), F32)


def row_pass(scalars, tgt, pot, src):
    half = pltpu.VMEM((1, src.shape[1] // 2), F32)
    ids, levels, counts = scalars
    slots = ids.shape[2]
    return pl.pallas_call(
        row_kernel,
        out_shape=(
            half,
            half,
            pltpu.VMEM((slots, tgt.shape[0], BLK), BF16),
            pltpu.VMEM((slots, 1, BLK), F32),
            pltpu.VMEM((slots, src.shape[0], BLK), BF16),
        ),
        in_specs=[pl.BlockSpec(memory_space=pltpu.HBM)] * 6,
        out_specs=(WHOLE,) * 5,
        scratch_shapes=[
            pltpu.SMEM(ids.shape, jnp.int32),
            pltpu.SMEM(levels.shape, jnp.int32),
            pltpu.SMEM(counts.shape, jnp.int32),
            pltpu.SemaphoreType.DMA((3,)),
            pltpu.SemaphoreType.DMA((3, slots)),
            pltpu.VMEM((1, src.shape[1]), F32),
            ROW,
        ]
        + [TGT_OPERAND, SRC_OPERAND, ROW] * 2,
        compiler_params=ROW_PARAMS,
        name="row_pass",
    )(ids, levels, counts, tgt, pot, src)


def col_pass(scalars, tgt, pot, src, own, other, columns):
    return pl.pallas_call(
        col_kernel,
        out_shape=jax.ShapeDtypeStruct((1, columns), F32),
        in_specs=[SCALAR] * 3 + [WHOLE] * 5,
        out_specs=WHOLE,
        scratch_shapes=[pltpu.VMEM((columns, LANES), F32)]
        + [TGT_OPERAND, SRC_OPERAND] * 2,
        compiler_params=PARAMS,
        name="col_pass",
    )(*scalars, tgt, pot, src, own, other)


def log_sum(parts):
    peak = functools.reduce(jnp.maximum, parts)
    return peak + jnp.log2(sum(jnp.exp2(part - peak) for part in parts))


def exchanged(value, axis, masks):
    size = lax.axis_size(axis)
    parts = [
        lax.ppermute(value, axis, [(i, i ^ mask) for i in range(size)]) for mask in masks
    ]
    return log_sum([value, *parts])


def local(src, tgt, pot, src_log, tgt_log, tile_ids, tile_level, tile_count):
    core = lax.axis_index("tgt") % 2
    scalars = (tile_ids, tile_level, tile_count)
    src_t, tgt_t = src.T, tgt.T
    kept, sent, *blocks = row_pass(scalars, tgt_t, pot[None], src_t)

    swap = [(i, i ^ 1) for i in range(lax.axis_size("tgt"))]
    half = log_sum([kept[0], lax.ppermute(sent[0], "tgt", swap)])
    half = exchanged(half, "tgt", (2, 4, 6))
    half = exchanged(half, "tgt", (8, 16, 24))
    src_half = lax.dynamic_index_in_dim(src_log.reshape(2, -1), core, 0, False)
    own = LOG2E * src_half - half
    other = lax.ppermute(own, "tgt", swap)

    col_lse = col_pass(scalars, *blocks, own[None], other[None], tgt.shape[0])[0]
    col_lse = exchanged(col_lse, "src", (1, 2, 3))
    col_lse = exchanged(col_lse, "src", (6,))
    new_pot = tgt_log + pot - (LN2 * (col_lse - UP) + 1.0)
    sp = jnp.where(core == 0, jnp.concatenate([own, other]), jnp.concatenate([other, own]))
    return LN2 * sp, new_pot


def solution(mesh):
    placed = (
        P("src", None),
        P("tgt", None),
        P("tgt"),
        P("src"),
        P("tgt"),
        P("src", "tgt", None),
        P("src", "tgt", None),
        P("src", "tgt"),
    )
    return jax.shard_map(
        local, mesh=mesh, in_specs=placed, out_specs=(P("src"), P("tgt")), check_vma=False
    )
```
